512 devices in a mesh: exp: 8 (over z), tp: 16 (over y, core), dp: 4 (over x).
Axes of the slice: x: 4, y: 8, z: 8, core: 2. Of those that a mesh axis runs over, the one named last changes fastest.
Arguments:
- tokens: bfloat16 [4096, 3072], P(('dp', 'exp', 'tp')), parts along dimension 0, may hold values from -6 to 6
- routes: int32 [4096, 2], P(('dp', 'exp')), parts along dimension 0, may hold values from 0 to 3, all different within a row; in each aligned block of 128 rows (0 to 127, 128 to 255, ...) at most 80 rows name the same one
- gates: float32 [4096, 2], P(('dp', 'exp')), parts along dimension 0, may hold values from 0.2 to 1
- w_gate: bfloat16 [8, 3072, 4096], P('exp', None, 'tp'), may hold values from -0.109375 to 0.109375
- w_up: bfloat16 [8, 3072, 4096], P('exp', None, 'tp'), may hold values from -0.109375 to 0.109375
- w_down: bfloat16 [8, 4096, 3072], P('exp', 'tp'), may hold values from -0.0625 to 0.0625
Outputs:
- mixed: bfloat16 [4096, 3072], P(('dp', 'exp', 'tp')), parts along dimension 0
The draws below stay inside these ranges and needn't reach their ends.
There are 4 independent parts, one for each index of `dp`. The reference program is written for one: setup_inputs(seed, part) draws one part's arguments, and reference() takes and returns one part's arrays. A program takes and returns all parts, laid end to end along the dimension named above; an argument that names none is the same for every part. Nothing has to cross between parts.
Inputs may be any that keep to these rules, and one draw needn't show every extreme that they name: `routes`: each token names two different experts; within the 128 tokens of one index of exp (aligned blocks of rows) no expert is named by more than 80 tokens, a bound that some blocks reach.
All inputs are finite; a program needn't handle non-finite values.
Results may differ from the reference program's by a relative error of at most 0.023.
Values may be sent and summed in bfloat16 or wider, within the bound.
A program may use at most 64 MiB of HBM per device.

```python
import math
import jax
import jax.numpy as jnp
import numpy as np
from jax import lax

D = 3072
FF = 8192
TOK_DEV = 8
EXPERTS = 4
GROUP = 2
FF_DEV = 256
TOKENS = 1024
CAP = 80
N_EXP = 8
N_TP = 16


def level_of(rng, shape, shards, smallest, high):
    factor_of = 1.0
    for dim, blocks in shards:
        heights = jax.random.uniform(jax.random.fold_in(jax.random.fold_in(rng, 6), dim), (blocks,), jnp.float32, smallest / len(shards), high / len(shards))
        factor_of = factor_of * jnp.repeat(jnp.exp(heights), shape[dim] // blocks).reshape((-1,) + (1,) * (len(shape) - 1 - dim))
    return factor_of


def assign_block(rng, own, number, rows, amount, top, most, lean):
    ranking = jax.random.permutation(rng, amount)
    heavy_load, ordinary = load_shares(amount, rows * top, most, lean, True), load_shares(amount, rows * top, most, lean, False)
    places = jnp.arange(amount)

    def named(lengths, turn):
        used = int((lengths > 0).sum())
        fixed = max(1, used // 4)
        moved = fixed + (places - fixed + turn * (used - fixed)) % max(1, amount - fixed)
        return jnp.zeros((amount,), jnp.int32).at[ranking[jnp.where(places < fixed, places, moved)]].set(jnp.asarray(lengths, jnp.int32))

    lengths = jnp.where(number % 4 == 0, named(heavy_load, number // 4), named(ordinary, number - number // 4 - 1))
    mixed = jax.random.permutation(jax.random.fold_in(own, 3), amount)
    giver, receiver = mixed[0:amount // 2 * 2:2], mixed[1:amount // 2 * 2:2]
    room = jnp.minimum(lengths[giver] - 1, most - lengths[receiver]) // 2
    room = jnp.where((giver == ranking[0]) | (receiver == ranking[0]) | (lengths[receiver] == 0), 0, jnp.maximum(room, 0))
    moved = jax.random.randint(jax.random.fold_in(own, 4), (amount // 2,), 0, 1 << 20) % (room + 1)
    lengths = lengths.at[giver].add(-moved).at[receiver].add(moved)
    members = jnp.searchsorted(jnp.cumsum(lengths), jnp.arange(rows * top), side="right").astype(jnp.int32)
    listing = members.reshape(top, rows).T
    listing = listing[jax.random.permutation(jax.random.fold_in(own, 1), rows)]
    turn = jax.random.randint(jax.random.fold_in(own, 2), (rows, 1), 0, top)
    return jnp.take_along_axis(listing, (jnp.arange(top)[None, :] + turn) % top, axis=1)


def load_shares(number_of, total, bound, skew, full):
    loads = [(1 << 20) // math.isqrt(grade ** skew) + 1 for grade in range(1, number_of + 1)]
    largest = bound if full else min(bound, max(-(-total // number_of), total * loads[0] // sum(loads)))
    least = 1 if total - largest >= number_of - 1 else 0
    counts, spare = [largest] + [least] * (number_of - 1), total - largest - least * (number_of - 1)
    while spare > 0:
        movable = [i for i in range(1, number_of) if counts[i] < largest] or [i for i in range(1, number_of) if counts[i] < bound]
        pool, left = sum([loads[i] for i in movable]), spare
        for i in movable:
            more = min(bound - counts[i], max(1, left * loads[i] // pool), spare)
            counts[i] = counts[i] + more
            spare = spare - more
    return np.array(counts)


def gaussian(own_key, shape, deviation, reach, pieces=(), held_as=jnp.bfloat16):
    factor_of = level_of(own_key, shape, pieces, -0.22, 0.18) if pieces else 1.0
    drawn = jax.random.normal(own_key, shape, jnp.float32) * deviation * factor_of
    return jnp.minimum(jnp.maximum(drawn, -reach), reach).astype(held_as)


def setup_inputs(seed: int = 0, part: int = 0) -> dict:
    key_of = jax.random.split(jax.random.key(seed), 7)
    own_keys = jax.random.split(jax.random.fold_in(key_of[6], part), 7)
    tokens = gaussian(own_keys[0], (TOKENS, D), 1.0, 6.0, ((0, 128),))
    routes_keys = jax.random.split(jax.random.fold_in(own_keys[1], 1), TOKENS // (TOK_DEV * N_TP))
    routes_turns = jax.random.permutation(jax.random.fold_in(own_keys[1], 3), TOKENS // (TOK_DEV * N_TP))
    routes = jax.vmap(lambda own, number: assign_block(jax.random.fold_in(own_keys[1], 2), own, number, TOK_DEV * N_TP, EXPERTS, 2, CAP, 2))(routes_keys, routes_turns).reshape((TOKENS, 2))
    gates = jnp.clip(0.2 + 0.8 * jax.random.uniform(own_keys[2], (TOKENS, 2), jnp.float32) ** level_of(own_keys[2], (TOKENS, 2), ((0, 8),), -0.2, 0.2), 0.2, 1.0)
    w_gate = gaussian(key_of[3], (EXPERTS * GROUP, D, FF // GROUP), D ** -0.5, 0.109375, ((0, 8), (2, 16)))
    w_up = gaussian(key_of[4], (EXPERTS * GROUP, D, FF // GROUP), D ** -0.5, 0.109375, ((0, 8), (2, 16)))
    w_down = gaussian(key_of[5], (EXPERTS * GROUP, FF // GROUP, D), FF ** -0.5, 0.0625, ((0, 8), (1, 16)))
    return {"tokens": tokens, "routes": routes, "gates": gates, "w_gate": w_gate, "w_up": w_up, "w_down": w_down}


def join_experts(weight, rows_last):
    group_size = N_EXP // EXPERTS
    if rows_last:
        shaped = weight.reshape(EXPERTS, group_size, D, FF // group_size)
        return shaped.transpose(0, 2, 1, 3).reshape(EXPERTS, D, FF)
    return weight.reshape(EXPERTS, FF, D)


def reference(tokens, routes, gates, w_gate, w_up, w_down):
    gate_all = join_experts(w_gate, True)
    up_all = join_experts(w_up, True)
    down_all = join_experts(w_down, False)
    blocks = FF // FF_DEV
    total = jnp.zeros((TOKENS, D), jnp.float32)
    for expert in range(EXPERTS):
        gate_proj = jnp.dot(tokens, gate_all[expert], preferred_element_type=jnp.float32)
        up_proj = jnp.dot(tokens, up_all[expert], preferred_element_type=jnp.float32)
        hidden = (jax.nn.silu(gate_proj) * up_proj).astype(jnp.bfloat16)
        down = down_all[expert]

        def add_block(carry_sum, index):
            begin = (index * FF_DEV).astype(jnp.int32)
            piece = lax.dynamic_slice_in_dim(hidden, begin, FF_DEV, 1)
            weights = lax.dynamic_slice_in_dim(down, begin, FF_DEV, 0)
            partial_value = jnp.dot(piece, weights, preferred_element_type=jnp.float32).astype(jnp.bfloat16)
            partial_value = lax.optimization_barrier(partial_value)
            return carry_sum + partial_value.astype(jnp.float32), None

        expert_out, _ = lax.scan(add_block, jnp.zeros((TOKENS, D), jnp.float32), jnp.arange(blocks, dtype=jnp.int32))
        weight_tok = jnp.sum(gates * (routes == expert).astype(jnp.float32), axis=1)
        total = total + weight_tok[:, None] * expert_out
    return total.astype(jnp.bfloat16)
```

```python
import functools

import jax
import jax.numpy as jnp
from jax import lax
from jax.experimental import pallas as pl
from jax.experimental.pallas import tpu as pltpu
from jax.sharding import PartitionSpec as P

MESH = pl.DeviceIdType.MESH
EXPERTS = 4
NZ = 8
NY = 8
NC = 2
ROWS = 128
CAP = 80
BLOCKS = NZ // NC
OFFSETS = ((0, 2, 6, 4), (1, 7, 3, 5))
STEPS = tuple((3, 4) if j % 2 == 0 else (4, 3) for j in range(BLOCKS))


def schedule():
    tasks = []
    for j in range(BLOCKS):
        start = 5.0 * j
        for h in range(1, 6):
            tasks.append((start + 2.7 * (h - 1), 0, "gather", j, h))
        full = start + 2.7 * 4
        tasks.append((full + 0.1, 1, "up", j, 0))
        tasks.append((full + 1.5, 2, "down", j, 0))
        for s in range(1, 6):
            tasks.append((full + 2.3 + 3.4 * (s - 1), 3, "scatter", j, s))
    tasks.sort()
    return [(kind, j, h) for _, _, kind, j, h in tasks]


def kernel(
    tok, routes_in, gates_in, wg, wu, wd, out,
    routes, gates, arrived, gate_w, up_w, down_w, hot, back_hot, weight, packed, rows, hidden, partial,
    leaving, coming, summed, returned, mixed, owned,
    p1s, p1r, lw, ws, wr, p3s, p3r, ags, agr, rss, rsr, rts, rtr, fs, fr,
):
    z = lax.axis_index("exp")
    t = lax.axis_index("tp")
    y = t // NC
    c = lax.rem(t, NC)
    home_core = lax.rem(z, NC)
    parity = lax.rem(z + c, NC)
    is_home = parity == 0
    share = rows.shape[-1]
    width = tok.shape[-1]

    def at(zz, yy, cc):
        return {"exp": zz, "tp": yy * NC + cc}

    def ring(v, n):
        return lax.rem(v + n, n)

    def send(src, dst, ssem, rsem, device):
        copy = pltpu.make_async_remote_copy(
            src_ref=src, dst_ref=dst, send_sem=ssem, recv_sem=rsem, device_id=device, device_id_type=MESH
        )
        copy.start()

    def sent(src, sem):
        pltpu.make_async_copy(src, src, sem).wait()

    def came(dst, sem):
        pltpu.make_async_copy(dst, dst, sem).wait()

    def chunk(ref, index):
        return ref.at[:, pl.ds(pl.multiple_of(index * share, 128), share)]

    weights = ((wg, gate_w), (wu, up_w), (wd, down_w))
    for i, (src, dst) in enumerate(weights):
        pltpu.make_async_copy(src.at[0], dst.at[c], lw.at[i]).start()

    routing = ((routes_in, routes), (gates_in, gates))
    for i, (src, dst) in enumerate(routing):
        pltpu.make_async_copy(src, dst, lw.at[3 + i]).start()

    barrier = pltpu.get_barrier_semaphore()
    for dy in range(NY):
        for dc in range(NC):
            if dy or dc:
                pl.semaphore_signal(
                    barrier, inc=1, device_id=at(z, ring(y + dy, NY), ring(c + dc, NC)), device_id_type=MESH
                )
    for dz in range(1, NZ):
        pl.semaphore_signal(barrier, inc=1, device_id=at(ring(z + dz, NZ), y, c), device_id_type=MESH)
    pl.semaphore_wait(barrier, NY * NC - 1 + NZ - 1)

    for dy in (4, 3, 5, 2, 6, 1, 7):
        to = ring(y + dy, NY)
        send(chunk(tok, to), arrived.at[t], p1s.at[dy], p1r.at[t], at(z, to, home_core))

    @pl.when(is_home)
    def _():
        pltpu.make_async_copy(chunk(tok, y), arrived.at[t], p1r.at[t]).start()

    @pl.when(jnp.logical_not(is_home))
    def _():
        send(chunk(tok, y), arrived.at[t], p1s.at[0], p1r.at[t], at(z, y, home_core))

    for i, (src, dst) in enumerate(weights):
        send(src.at[0], dst.at[c], ws.at[i], wr.at[i], at(z, y, 1 - c))

    for i, (src, dst) in enumerate(routing):
        came(dst, lw.at[3 + i])

    def pick(e, first, second):
        here = [jnp.broadcast_to(routes[k:k + 1, :], (ROWS, ROWS)) == e for k in range(2)]
        return jnp.where(here[0], first, 0.0) + jnp.where(here[1], second, 0.0)

    @pl.when(is_home)
    def _():
        row_ids = lax.broadcasted_iota(jnp.int32, (ROWS, ROWS), 0)
        col_ids = lax.broadcasted_iota(jnp.int32, (ROWS, ROWS), 1)
        earlier = jnp.where(row_ids < col_ids, 1.0, 0.0).astype(jnp.bfloat16)
        slots = row_ids.astype(jnp.float32)
        g0, g1 = (jnp.broadcast_to(gates[k:k + 1, :], (ROWS, ROWS)) for k in range(2))
        for e in range(EXPERTS):
            mine = pick(e, 1.0, 1.0)
            before = jnp.dot(mine.astype(jnp.bfloat16), earlier, preferred_element_type=jnp.float32)
            placed = jnp.where(before == slots, mine, 0.0)
            hot[e] = placed.astype(jnp.bfloat16)
            back_hot[e] = placed.T.astype(jnp.bfloat16)
            gate = jnp.sum(jnp.where(row_ids == col_ids, pick(e, g0, g1), 0.0), axis=1, keepdims=True)
            weight[e] = jnp.broadcast_to(gate, (ROWS, 128))
        for i in range(NY * NC):
            came(arrived.at[i], p1r.at[i])
        block = arrived[...].astype(jnp.float32).reshape(ROWS, share).astype(jnp.bfloat16)
        for e in range(EXPERTS):
            packed[e] = jnp.dot(hot[e, :CAP, :], block, preferred_element_type=jnp.float32).astype(jnp.bfloat16)
        for j in range(BLOCKS):
            for side in range(2):
                d = (NZ - OFFSETS[side][j]) % NZ
                to = ring(z + d, NZ)
                src = packed.at[to // (NZ // EXPERTS)]
                if d == 0:
                    pltpu.make_async_copy(src, rows.at[j, y], p3r.at[j]).start()
                else:
                    send(src, rows.at[j, y], p3s.at[d], p3r.at[j], at(to, y, c))

    def gather(j, h):
        if h == 1:
            came(rows.at[j, y], p3r.at[j])
        for way, sign in ((0, 1), (1, -1)):
            count = STEPS[j][way]
            if 2 <= h <= count + 1:
                came(rows.at[j, ring(y - sign * (h - 1), NY)], agr.at[j, way, h - 2])
            if h <= count:
                piece = rows.at[j, ring(y - sign * (h - 1), NY)]
                send(piece, piece, ags.at[j, way, h - 1], agr.at[j, way, h - 1], at(z, ring(y + sign, NY), c))

    def up(j):
        if j == 0:
            for i, (src, dst) in enumerate(weights[:2]):
                came(dst.at[c], lw.at[i])
                came(dst.at[1 - c], wr.at[i])
        x = jnp.concatenate([rows[j, f] for f in range(NY)], axis=1)
        for core in range(NC):
            g = jnp.dot(x, gate_w[core], preferred_element_type=jnp.float32)
            u = jnp.dot(x, up_w[core], preferred_element_type=jnp.float32)
            n = g.shape[1]
            hidden[j, :, core * n:(core + 1) * n] = (g / (1.0 + jnp.exp(-g)) * u).astype(jnp.bfloat16)

    def down(j):
        if j == 0:
            came(down_w.at[c], lw.at[2])
            came(down_w.at[1 - c], wr.at[2])
        n = down_w.shape[1]
        for f in range(0, NY, 2):
            lo, hi = f * share, (f + 2) * share
            r = jnp.dot(hidden[j, :, :n], down_w[0, :, lo:hi], preferred_element_type=jnp.float32)
            r += jnp.dot(hidden[j, :, n:], down_w[1, :, lo:hi], preferred_element_type=jnp.float32)
            partial[j, f] = r[:, :share]
            partial[j, f + 1] = r[:, share:]

    def scatter(j, s):
        for way, sign in ((0, 1), (1, -1)):
            count = STEPS[j][way]
            if s > count:
                continue
            piece = partial[j, ring(y + sign * (count - s + 1), NY)]
            if s >= 2:
                came(coming.at[j, way, s - 2], rsr.at[j, way, s - 2])
                piece = piece + coming[j, way, s - 2].astype(jnp.float32)
            leaving[j, way, s - 1] = piece.astype(jnp.bfloat16)
            send(
                leaving.at[j, way, s - 1], coming.at[j, way, s - 1], rss.at[j, way, s - 1], rsr.at[j, way, s - 1],
                at(z, ring(y + sign, NY), c),
            )
        if s == 5:
            total = partial[j, y]
            for way in range(2):
                last = STEPS[j][way] - 1
                came(coming.at[j, way, last], rsr.at[j, way, last])
                total = total + coming[j, way, last].astype(jnp.float32)
            summed[j] = total.astype(jnp.bfloat16)
            back = ring(z + OFFSETS[0][j] + parity * (OFFSETS[1][j] - OFFSETS[0][j]), NZ)
            if j == 0:
                @pl.when(is_home)
                def _():
                    pltpu.make_async_copy(summed.at[j], returned.at[z], rtr.at[z]).start()

                @pl.when(jnp.logical_not(is_home))
                def _():
                    send(summed.at[j], returned.at[z], rts.at[j], rtr.at[z], at(back, y, c))
            else:
                send(summed.at[j], returned.at[z], rts.at[j], rtr.at[z], at(back, y, c))

    for kind, j, h in schedule():
        if kind == "gather":
            gather(j, h)
        elif kind == "up":
            up(j)
        elif kind == "down":
            down(j)
        else:
            scatter(j, h)

    @pl.when(is_home)
    def _():
        for i in range(NZ):
            came(returned.at[i], rtr.at[i])
        total = jnp.zeros((ROWS, share), jnp.float32)
        for e in range(EXPERTS):
            picked = jnp.zeros((ROWS, share), jnp.float32)
            for g in range(NZ // EXPERTS):
                picked += jnp.dot(
                    back_hot[e, :, :CAP], returned[e * (NZ // EXPERTS) + g], preferred_element_type=jnp.float32
                )
            total += jnp.concatenate([weight[e]] * (share // 128), axis=1) * picked
        mixed[...] = total.reshape(NY * NC, ROWS // (NY * NC), share).astype(jnp.bfloat16)
        for dy in (4, 3, 5, 2, 6, 1, 7, 0):
            for dc in range(NC):
                to, core = ring(y + dy, NY), ring(c + dc, NC)
                src = mixed.at[to * NC + core]
                if dy == 0 and dc == 0:
                    pltpu.make_async_copy(src, chunk(owned, y), fr.at[y]).start()
                else:
                    send(src, chunk(owned, y), fs.at[dy * NC + dc], fr.at[y], at(z, to, core))

    for i in range(NY):
        came(owned.at[:, i * share:(i + 1) * share], fr.at[i])
    out[...] = owned[...]

    for dy in range(1, NY):
        sent(chunk(tok, y), p1s.at[dy])
    for i, (src, dst) in enumerate(weights):
        sent(src.at[0], ws.at[i])
    for j in range(BLOCKS):
        for way in range(2):
            for h in range(STEPS[j][way]):
                sent(rows.at[j, 0], ags.at[j, way, h])
                sent(leaving.at[j, way, h], rss.at[j, way, h])
        if j > 0:
            sent(summed.at[j], rts.at[j])

    @pl.when(is_home)
    def _():
        for d in range(1, NZ):
            sent(packed.at[0], p3s.at[d])
        for i in range(1, NY * NC):
            sent(mixed.at[0], fs.at[i])

    @pl.when(jnp.logical_not(is_home))
    def _():
        sent(chunk(tok, y), p1s.at[0])
        sent(summed.at[0], rts.at[0])


def local(tokens, routes, gates, w_gate, w_up, w_down):
    tok_dev, width = tokens.shape
    hid = w_gate.shape[2]
    share = width // NY
    bf16, f32 = jnp.bfloat16, jnp.float32
    vmem = pl.BlockSpec(memory_space=pltpu.VMEM)
    hbm = pl.BlockSpec(memory_space=pltpu.HBM)
    dma = pltpu.SemaphoreType.DMA
    return pl.pallas_call(
        kernel,
        out_shape=jax.ShapeDtypeStruct((tok_dev, width), bf16),
        in_specs=[hbm] * 6,
        out_specs=vmem,
        scratch_shapes=[
            pltpu.VMEM((2, ROWS), jnp.int32),
            pltpu.VMEM((2, ROWS), f32),
            pltpu.VMEM((NY * NC, tok_dev, share), bf16),
            pltpu.VMEM((NC, width, hid), bf16),
            pltpu.VMEM((NC, width, hid), bf16),
            pltpu.VMEM((NC, hid, width), bf16),
            pltpu.VMEM((EXPERTS, ROWS, ROWS), bf16),
            pltpu.VMEM((EXPERTS, ROWS, ROWS), bf16),
            pltpu.VMEM((EXPERTS, ROWS, 128), f32),
            pltpu.VMEM((EXPERTS, CAP, share), bf16),
            pltpu.VMEM((BLOCKS, NY, CAP, share), bf16),
            pltpu.VMEM((BLOCKS, CAP, NC * hid), bf16),
            pltpu.VMEM((BLOCKS, NY, CAP, share), f32),
            pltpu.VMEM((BLOCKS, 2, 4, CAP, share), bf16),
            pltpu.VMEM((BLOCKS, 2, 4, CAP, share), bf16),
            pltpu.VMEM((BLOCKS, CAP, share), bf16),
            pltpu.VMEM((NZ, CAP, share), bf16),
            pltpu.VMEM((NY * NC, tok_dev, share), bf16),
            pltpu.VMEM((tok_dev, width), bf16),
            dma((NY,)), dma((NY * NC,)),
            dma((5,)), dma((3,)), dma((3,)),
            dma((NZ,)), dma((BLOCKS,)),
            dma((BLOCKS, 2, 4)), dma((BLOCKS, 2, 4)),
            dma((BLOCKS, 2, 4)), dma((BLOCKS, 2, 4)),
            dma((BLOCKS,)), dma((NZ,)),
            dma((NY * NC,)), dma((NY,)),
        ],
        compiler_params=pltpu.CompilerParams(
            collective_id=0, has_side_effects=True, vmem_limit_bytes=62 * 2**20
        ),
        name="moe",
    )(tokens, routes.T, gates.T, w_gate, w_up, w_down)


def solution(mesh):
    return jax.shard_map(
        local,
        mesh=mesh,
        in_specs=(
            P(("dp", "exp", "tp"), None),
            P(("dp", "exp"), None),
            P(("dp", "exp"), None),
            P("exp", None, "tp"),
            P("exp", None, "tp"),
            P("exp", "tp", None),
        ),
        out_specs=P(("dp", "exp", "tp"), None),
        check_vma=False,
    )
```

```python
import jax
import jax.numpy as jnp
from jax import lax
from jax.experimental import pallas as pl
from jax.experimental.pallas import tpu as pltpu
from jax.sharding import PartitionSpec as P

MESH = pl.DeviceIdType.MESH
EXPERTS = 4
NZ = 8
NY = 8
NC = 2
ROWS = 128
CAP = 80
BLOCKS = NZ // NC
OFFSETS = ((0, 2, -2, 4), (1, 3, -1, -3))


GROUPS = ((0, 2), (1, 3))
GATHER = (((0, 1, 2, 3), (0,)), ((0, 0, 2, 3), (0,)), ((0,), (0, 1, 2, 3)), ((0,), (0, 0, 2, 3)))
SCATTER = (((0, 1, 2, 3), (0,)), ((0, 0, 2, 3), (0,)), ((0,), (0, 1, 2, 3)), ((0,), (0, 0, 2, 3)))
ORDER = (
    ("ag", 0, 0, 1),
    ("ag", 0, 1, 1),
    ("zo", 0),
    ("zo", 1),
    ("ag", 1, 1, 1),
    ("ag", 0, 0, 2),
    ("ag", 2, 1, 1),
    ("ag", 1, 0, 2),
    ("ag", 3, 1, 2),
    ("zf", 1, (0, 2)),
    ("ag", 1, 0, 3),
    ("ag", 2, 1, 2),
    ("ag", 1, 0, 1),
    ("zf", 0, (0, 2)),
    ("ag", 3, 1, 3),
    ("ag", 0, 0, 3),
    ("zf", 3, (1, 2)),
    ("ag", 2, 1, 3),
    ("zf", 1, (0, 3)),
    ("ag", 3, 1, 1),
    ("ag", 1, 0, 4),
    ("zf", 3, (1, 3)),
    ("ag", 3, 0, 1),
    ("ag", 3, 1, 4),
    ("ag", 2, 1, 4),
    ("zf", 0, (0, 3)),
    ("zf", 2, (1, 2)),
    ("zf", 2, (1, 3)),
    ("ag", 0, 0, 4),
    ("ag", 2, 0, 1),
    ("up", 1, 0),
    ("up", 1, 1),
    ("down", 1, 0),
    ("down", 1, 1),
    ("zs", 3, (0, 3)),
    ("rs", 3, 1, 4),
    ("rs", 1, 0, 4),
    ("zs", 1, (1, 3)),
    ("rs", 3, 0, 1),
    ("zs", 3, (0, 2)),
    ("rs", 1, 1, 1),
    ("up", 0, 0),
    ("up", 0, 1),
    ("down", 0, 0),
    ("down", 0, 1),
    ("rs", 2, 1, 4),
    ("zs", 0, (1, 3)),
    ("rs", 0, 0, 4),
    ("zs", 2, (0, 3)),
    ("rs", 0, 1, 1),
    ("rs", 1, 0, 1),
    ("rs", 1, 0, 3),
    ("zs", 0, (1, 2)),
    ("rs", 3, 1, 3),
    ("zs", 1, (1, 2)),
    ("rs", 2, 1, 3),
    ("rs", 0, 0, 3),
    ("zs", 2, (0, 2)),
    ("rs", 1, 0, 2),
    ("rs", 3, 1, 1),
    ("rs", 2, 1, 2),
    ("rs", 3, 1, 2),
    ("rs", 0, 0, 2),
    ("fin", 1),
    ("rs", 2, 0, 1),
    ("rs", 2, 1, 1),
    ("rs", 0, 0, 1),
    ("fin", 3),
    ("fin", 2),
    ("fin", 0),
)


def missing(mine, other):
    if sum(map(len, mine)) == NY - 1:
        return []
    return [
        (w, d) for w in range(2) for d in range(len(mine[w]) + 1, len(other[w]) + 1)
        if not (d == NY // 2 and len(mine[1 - w]) == d)
    ]


def kernel(
    tok_in, routes_in, gates_in, wg, wu, wd, out,
    tok, routes, gates, arrived, gate_w, up_w, down_w, hot, back_hot, weight, packed, rows, hidden, partial,
    leaving, coming, leaving_z, coming_z, summed, returned, mixed, owned,
    p1s, p1r, lw, ws, wr, p3s, p3r, zos, ags, agr, zfs, zfr, rss, rsr, zss, zsr, rts, rtr, fs, fr,
):
    groups, ag, rs, order = GROUPS, GATHER, SCATTER, ORDER
    z = lax.axis_index("exp")
    t = lax.axis_index("tp")
    y = t // NC
    c = lax.rem(t, NC)
    home_core = lax.rem(z, NC)
    side = lax.rem(z + c, NC)
    is_home = side == 0
    turn = 2 * home_core - 1
    share = rows.shape[-1]

    def at(zz, yy, cc):
        return {"exp": zz, "tp": yy * NC + cc}

    def ring(v, n):
        return lax.rem(v + n, n)

    def send(src, dst, ssem, rsem, device):
        pltpu.make_async_remote_copy(
            src_ref=src, dst_ref=dst, send_sem=ssem, recv_sem=rsem, device_id=device, device_id_type=MESH
        ).start()

    def wait(ref, sem):
        pltpu.make_async_copy(ref, ref, sem).wait()

    def chunk(ref, index):
        return ref.at[:, pl.ds(pl.multiple_of(index * share, 128), share)]

    partner = z - turn
    weights = ((wg, gate_w), (wu, up_w), (wd, down_w))
    small = ((tok_in, tok), (routes_in, routes), (gates_in, gates))
    for i, (src, dst) in enumerate(small):
        pltpu.make_async_copy(src, dst, lw.at[3 + i]).start()
    barrier = pltpu.get_barrier_semaphore()
    for dy in (4, 3, 5, 2, 6, 1, 7, 0):
        for dc in range(NC):
            if dy or dc:
                pl.semaphore_signal(
                    barrier, inc=1, device_id=at(z, ring(y + dy, NY), ring(c + dc, NC)), device_id_type=MESH
                )
    for dz in (4, 3, 5, 2, 6, 1, 7):
        pl.semaphore_signal(barrier, inc=1, device_id=at(ring(z + dz, NZ), y, c), device_id_type=MESH)
    for i, (src, dst) in enumerate(weights):
        pltpu.make_async_copy(src.at[0], dst.at[c], lw.at[i]).start()
    wait(tok, lw.at[3])
    pl.semaphore_wait(barrier, NY * NC - 1 + NZ - 1)

    for dy in (4, 3, 5, 2, 6, 1, 7):
        to = ring(y + dy, NY)
        send(chunk(tok, to), arrived.at[t], p1s.at[dy], p1r.at[t], at(z, to, home_core))

    @pl.when(is_home)
    def _():
        pltpu.make_async_copy(chunk(tok, y), arrived.at[t], p1r.at[t]).start()

    @pl.when(jnp.logical_not(is_home))
    def _():
        send(chunk(tok, y), arrived.at[t], p1s.at[0], p1r.at[t], at(z, y, home_core))

    for i, (src, dst) in enumerate(weights):
        send(src.at[0], dst.at[c], ws.at[i], wr.at[i], at(z, y, 1 - c))

    for i, (src, dst) in enumerate(small[1:]):
        wait(dst, lw.at[4 + i])

    def pick(e, first, second):
        here = [jnp.broadcast_to(routes[k:k + 1, :], (ROWS, ROWS)) == e for k in range(2)]
        return jnp.where(here[0], first, 0.0) + jnp.where(here[1], second, 0.0)

    @pl.when(is_home)
    def _():
        row_ids = lax.broadcasted_iota(jnp.int32, (ROWS, ROWS), 0)
        col_ids = lax.broadcasted_iota(jnp.int32, (ROWS, ROWS), 1)
        earlier = jnp.where(row_ids < col_ids, 1.0, 0.0).astype(jnp.bfloat16)
        slots = row_ids.astype(jnp.float32)
        for e in range(EXPERTS):
            mine = pick(e, 1.0, 1.0)
            before = jnp.dot(mine.astype(jnp.bfloat16), earlier, preferred_element_type=jnp.float32)
            placed = jnp.where(before == slots, mine, 0.0)
            hot[e] = placed.astype(jnp.bfloat16)
        for i in range(NY * NC):
            wait(arrived.at[i], p1r.at[i])
        block = arrived[...].astype(jnp.float32).reshape(ROWS, share).astype(jnp.bfloat16)
        for j, k in ((0, 0), (1, 1), (1, 0), (0, 1)):
            to = ring(z - turn * OFFSETS[0][j], NZ) if k == 0 else ring(z + turn * OFFSETS[1][j], NZ)
            e = to // (NZ // EXPERTS)
            packed[2 * k + j] = jnp.dot(hot[e, :CAP, :], block, preferred_element_type=jnp.float32).astype(jnp.bfloat16)
            if k == 0 and j == 0:
                pltpu.make_async_copy(packed.at[0], rows.at[j, y], p3r.at[j]).start()
            else:
                send(packed.at[2 * k + j], rows.at[j, y], p3s.at[2 * k + j], p3r.at[j], at(to, y, c))

    waited = set()

    def need(kind, j, *where):
        key = (kind, j) + where
        if key in waited:
            return
        waited.add(key)
        if kind == "p3":
            wait(rows.at[j, y], p3r.at[j])
        elif kind == "ag":
            way, h = where
            wait(rows.at[j, ring(y - (1 - 2 * way) * h, NY)], agr.at[j, way, h - 1])
        elif kind == "zf":
            (way, d), i = where
            wait(rows.at[j, ring(y - (1 - 2 * way) * d, NY)], zfr.at[j, i])
        elif kind == "rs":
            way, s = where
            wait(coming.at[j, way, s - 1], rsr.at[j, way, s - 1])
        elif kind == "zs":
            wait(coming_z.at[j, where[0]], zsr.at[j, where[0]])

    def gather(j, way, d):
        sign, parent = 1 - 2 * way, ag[j][way][d - 1]
        piece = rows.at[j, ring(y - sign * parent, NY)]
        need("ag", j, way, parent) if parent else need("p3", j)
        send(
            piece, piece, ags.at[j, way, d - 1], agr.at[j, way, d - 1],
            at(z, ring(y + sign * (d - parent), NY), c),
        )

    def share_own(j):
        need("p3", j)
        send(rows.at[j, y], rows.at[j ^ 2, y], zos.at[j], p3r.at[j ^ 2], at(partner, y, c))

    def forward(j, far):
        other = j ^ 2
        i = missing(ag[other], ag[j]).index(far)
        need("ag", j, *far)
        f = ring(y - (1 - 2 * far[0]) * far[1], NY)
        send(rows.at[j, f], rows.at[other, f], zfs.at[j, i], zfr.at[other, i], at(partner, y, c))

    def up(g, core):
        if core == 0:
            for j in groups[g]:
                need("p3", j)
                for way in range(2):
                    for h in range(1, len(ag[j][way]) + 1):
                        need("ag", j, way, h)
                for i, far in enumerate(missing(ag[j], ag[j ^ 2])):
                    need("zf", j, far, i)
        if "up" not in waited:
            waited.add("up")
            for i, (src, dst) in enumerate(weights[:2]):
                wait(dst.at[c], lw.at[i])
                wait(dst.at[1 - c], wr.at[i])
        x = jnp.concatenate(
            [jnp.concatenate([rows[j, f] for f in range(NY)], axis=1) for j in groups[g]], axis=0
        )
        gp = jnp.dot(x, gate_w[core], preferred_element_type=jnp.float32)
        u = jnp.dot(x, up_w[core], preferred_element_type=jnp.float32)
        n = gp.shape[1]
        hid = (gp / (1.0 + jnp.exp(-gp)) * u).astype(jnp.bfloat16)
        for i, j in enumerate(groups[g]):
            hidden[j, :, core * n:(core + 1) * n] = hid[i * CAP:(i + 1) * CAP]

    def down(g, half):
        if "down" not in waited:
            waited.add("down")
            wait(down_w.at[c], lw.at[2])
            wait(down_w.at[1 - c], wr.at[2])
        n = down_w.shape[1]
        h = jnp.concatenate([hidden[j] for j in groups[g]], axis=0)
        for f in range(half * NY // 2, (half + 1) * NY // 2, 2):
            lo, hi = f * share, (f + 2) * share
            r = jnp.dot(h[:, :n], down_w[0, :, lo:hi], preferred_element_type=jnp.float32)
            r += jnp.dot(h[:, n:], down_w[1, :, lo:hi], preferred_element_type=jnp.float32)
            for i, j in enumerate(groups[g]):
                partial[j, f] = r[i * CAP:(i + 1) * CAP, :share]
                partial[j, f + 1] = r[i * CAP:(i + 1) * CAP, share:]

    def across(j, far):
        other = j ^ 2
        i = missing(rs[j], rs[other]).index(far)
        f = ring(y + (1 - 2 * far[0]) * far[1], NY)
        leaving_z[j, i] = partial[j, f].astype(jnp.bfloat16)
        send(leaving_z.at[j, i], coming_z.at[other, i], zss.at[j, i], zsr.at[other, i], at(partner, y, c))

    def scatter(j, way, d):
        sign, parent = 1 - 2 * way, rs[j][way][d - 1]
        total = partial[j, ring(y + sign * d, NY)]
        far = missing(rs[j ^ 2], rs[j])
        if (way, d) in far:
            i = far.index((way, d))
            need("zs", j, i)
            total = total + coming_z[j, i].astype(jnp.float32)
        total = total + children(j, way, d)
        leaving[j, way, d - 1] = total.astype(jnp.bfloat16)
        send(
            leaving.at[j, way, d - 1], coming.at[j, way, d - 1], rss.at[j, way, d - 1], rsr.at[j, way, d - 1],
            at(z, ring(y + sign * (d - parent), NY), c),
        )

    def children(j, way, d):
        total = 0.0
        for e, parent in enumerate(rs[j][way], 1):
            if parent == d:
                need("rs", j, way, e)
                total = total + coming[j, way, e - 1].astype(jnp.float32)
        return total

    def finish(j):
        total = partial[j, y]
        for way in range(2):
            total = total + children(j, way, 0)
        summed[j] = total.astype(jnp.bfloat16)
        back = ring(z + turn * (OFFSETS[0][j] + side * (OFFSETS[1][j] - OFFSETS[0][j])), NZ)
        if j == 0:
            @pl.when(is_home)
            def _():
                pltpu.make_async_copy(summed.at[j], returned.at[z], rtr.at[z]).start()

            @pl.when(jnp.logical_not(is_home))
            def _():
                send(summed.at[j], returned.at[z], rts.at[j], rtr.at[z], at(back, y, c))
        else:
            send(summed.at[j], returned.at[z], rts.at[j], rtr.at[z], at(back, y, c))

    step = {"ag": gather, "zo": share_own, "zf": forward, "up": up, "down": down, "zs": across, "rs": scatter, "fin": finish}
    for task in order:
        step[task[0]](*task[1:])

    @pl.when(is_home)
    def _():
        diagonal = lax.broadcasted_iota(jnp.int32, (ROWS, ROWS), 0) == lax.broadcasted_iota(jnp.int32, (ROWS, ROWS), 1)
        g0, g1 = (jnp.broadcast_to(gates[k:k + 1, :], (ROWS, ROWS)) for k in range(2))
        for e in range(EXPERTS):
            back_hot[e] = hot[e].astype(jnp.float32).T.astype(jnp.bfloat16)
            gate = jnp.sum(jnp.where(diagonal, pick(e, g0, g1), 0.0), axis=1, keepdims=True)
            weight[e] = jnp.broadcast_to(gate, (ROWS, 128))
        total = jnp.zeros((ROWS, share), jnp.float32)
        for j in [task[1] for task in order if task[0] == "fin"]:
            for k in range(2):
                to = ring(z - turn * OFFSETS[0][j], NZ) if k == 0 else ring(z + turn * OFFSETS[1][j], NZ)
                e = to // (NZ // EXPERTS)
                wait(returned.at[to], rtr.at[to])
                picked = jnp.dot(back_hot[e, :, :CAP], returned[to], preferred_element_type=jnp.float32)
                total += jnp.concatenate([weight[e]] * (share // 128), axis=1) * picked
        mixed[...] = total.reshape(NY * NC, ROWS // (NY * NC), share).astype(jnp.bfloat16)
        for dy in (4, 3, 5, 2, 6, 1, 7, 0):
            for dc in range(NC):
                to, core = ring(y + dy, NY), ring(c + dc, NC)
                src = mixed.at[to * NC + core]
                if dy == 0 and dc == 0:
                    pltpu.make_async_copy(src, chunk(owned, y), fr.at[y]).start()
                else:
                    send(src, chunk(owned, y), fs.at[dy * NC + dc], fr.at[y], at(z, to, core))

    for dy in range(1, NY):
        wait(chunk(tok, y), p1s.at[dy])
    for i, (src, dst) in enumerate(weights):
        wait(src.at[0], ws.at[i])
    for j in range(BLOCKS):
        for way in range(2):
            for h in range(len(ag[j][way])):
                wait(rows.at[j, 0], ags.at[j, way, h])
            for h in range(len(rs[j][way])):
                wait(leaving.at[j, way, h], rss.at[j, way, h])
        for i in range(len(missing(ag[j ^ 2], ag[j]))):
            wait(rows.at[j, 0], zfs.at[j, i])
        for i in range(len(missing(rs[j], rs[j ^ 2]))):
            wait(leaving_z.at[j, i], zss.at[j, i])
        if j > 0:
            wait(summed.at[j], rts.at[j])
        if j < 2:
            wait(rows.at[j, 0], zos.at[j])

    @pl.when(is_home)
    def _():
        for i in range(1, 4):
            wait(packed.at[0], p3s.at[i])
        for i in range(1, NY * NC):
            wait(mixed.at[0], fs.at[i])

    @pl.when(jnp.logical_not(is_home))
    def _():
        wait(chunk(tok, y), p1s.at[0])
        wait(summed.at[0], rts.at[0])

    for i in range(NY):
        wait(owned.at[:, i * share:(i + 1) * share], fr.at[i])
    out[...] = owned[...]


def local(tokens, routes, gates, w_gate, w_up, w_down):
    tok_dev, width = tokens.shape
    hid = w_gate.shape[2]
    share = width // NY
    bf16, f32 = jnp.bfloat16, jnp.float32
    dma = pltpu.SemaphoreType.DMA
    hbm = pl.BlockSpec(memory_space=pltpu.HBM)
    return pl.pallas_call(
        kernel,
        out_shape=jax.ShapeDtypeStruct((tok_dev, width), bf16),
        in_specs=[hbm] * 6,
        out_specs=pl.BlockSpec(memory_space=pltpu.VMEM),
        scratch_shapes=[
            pltpu.VMEM((tok_dev, width), bf16),
            pltpu.VMEM((2, ROWS), jnp.int32),
            pltpu.VMEM((2, ROWS), f32),
            pltpu.VMEM((NY * NC, tok_dev, share), bf16),
            pltpu.VMEM((NC, width, hid), bf16),
            pltpu.VMEM((NC, width, hid), bf16),
            pltpu.VMEM((NC, hid, width), bf16),
            pltpu.VMEM((EXPERTS, ROWS, ROWS), bf16),
            pltpu.VMEM((EXPERTS, ROWS, ROWS), bf16),
            pltpu.VMEM((EXPERTS, ROWS, 128), f32),
            pltpu.VMEM((EXPERTS, CAP, share), bf16),
            pltpu.VMEM((BLOCKS, NY, CAP, share), bf16),
            pltpu.VMEM((BLOCKS, CAP, NC * hid), bf16),
            pltpu.VMEM((BLOCKS, NY, CAP, share), f32),
            pltpu.VMEM((BLOCKS, 2, 4, CAP, share), bf16),
            pltpu.VMEM((BLOCKS, 2, 4, CAP, share), bf16),
            pltpu.VMEM((BLOCKS, 3, CAP, share), bf16),
            pltpu.VMEM((BLOCKS, 3, CAP, share), bf16),
            pltpu.VMEM((BLOCKS, CAP, share), bf16),
            pltpu.VMEM((NZ, CAP, share), bf16),
            pltpu.VMEM((NY * NC, tok_dev, share), bf16),
            pltpu.VMEM((tok_dev, width), bf16),
            dma((NY,)), dma((NY * NC,)),
            dma((6,)), dma((3,)), dma((3,)),
            dma((4,)), dma((BLOCKS,)), dma((2,)),
            dma((BLOCKS, 2, 4)), dma((BLOCKS, 2, 4)),
            dma((BLOCKS, 3)), dma((BLOCKS, 3)),
            dma((BLOCKS, 2, 4)), dma((BLOCKS, 2, 4)),
            dma((BLOCKS, 3)), dma((BLOCKS, 3)),
            dma((BLOCKS,)), dma((NZ,)),
            dma((NY * NC,)), dma((NY,)),
        ],
        compiler_params=pltpu.CompilerParams(
            collective_id=0, has_side_effects=True, vmem_limit_bytes=62 * 2**20
        ),
        name="moe",
    )(tokens, routes.T, gates.T, w_gate, w_up, w_down)


def solution(mesh):
    return jax.shard_map(
        local,
        mesh=mesh,
        in_specs=(
            P(("dp", "exp", "tp"), None),
            P(("dp", "exp"), None),
            P(("dp", "exp"), None),
            P("exp", None, "tp"),
            P("exp", None, "tp"),
            P("exp", "tp", None),
        ),
        out_specs=P(("dp", "exp", "tp"), None),
        check_vma=False,
    )
```

```python
import jax
import jax.numpy as jnp
from jax import lax
from jax.experimental import pallas as pl
from jax.experimental.pallas import tpu as pltpu
from jax.sharding import PartitionSpec as P

MESH = pl.DeviceIdType.MESH
EXPERTS = 4
NZ = 8
NY = 8
NC = 2
ROWS = 128
CAP = 80
BLOCKS = NZ // NC
OFFSETS = ((0, 2, -2, 4), (1, 3, -1, -3))


HEAVY = (0, 1, 0, 1)


GROUPS = ((0, 2), (1, 3))
GATHER = (((0, 1, 2), (0, 1)), ((0, 1), (0, 1, 2)), ((0, 1, 2), (0, 1)), ((0, 1), (0, 1, 2)))
SCATTER = (((0, 1, 2), (0, 1)), ((0, 1), (0, 1, 2)), ((0, 1, 2), (0, 1)), ((0, 1), (0, 1, 2)))
ORDER = (
    ("ag", 0, 0, 1),
    ("ag", 0, 1, 1),
    ("ag", 2, 1, 1),
    ("ag", 2, 0, 1),
    ("ag", 0, 0, 2),
    ("zc", 2),
    ("ag", 1, 1, 1),
    ("ag", 2, 0, 2),
    ("ag", 1, 0, 1),
    ("ag", 2, 1, 2),
    ("zf", 2),
    ("zf", 0),
    ("ag", 3, 1, 1),
    ("prep",),
    ("zc", 0),
    ("ag", 0, 0, 3),
    ("ag", 2, 0, 3),
    ("ag", 0, 1, 2),
    ("ag", 3, 1, 2),
    ("ag", 1, 1, 2),
    ("zf", 1),
    ("zc", 1),
    ("ag", 3, 0, 1),
    ("zc", 3),
    ("zf", 3),
    ("up", 0, 0),
    ("ag", 1, 0, 2),
    ("ag", 3, 1, 3),
    ("ag", 1, 1, 3),
    ("ag", 3, 0, 2),
    ("up", 0, 1),
    ("down", 0, 0),
    ("down", 0, 1),
    ("rs", 2, 1, 2),
    ("rs", 0, 0, 3),
    ("zt", 0),
    ("rs", 0, 1, 2),
    ("rs", 2, 0, 3),
    ("up", 1, 0),
    ("up", 1, 1),
    ("down", 1, 0),
    ("down", 1, 1),
    ("rs", 3, 1, 3),
    ("rs", 1, 0, 2),
    ("rs", 1, 1, 3),
    ("zs", 0),
    ("rs", 3, 0, 2),
    ("rs", 2, 0, 2),
    ("zs", 1),
    ("rs", 3, 1, 2),
    ("zs", 3),
    ("rs", 1, 1, 2),
    ("rs", 3, 0, 1),
    ("zt", 1),
    ("zs", 2),
    ("rs", 0, 0, 2),
    ("rs", 3, 1, 1),
    ("rs", 2, 0, 1),
    ("rs", 2, 1, 1),
    ("rs", 1, 0, 1),
    ("zt", 3),
    ("rs", 1, 1, 1),
    ("fin", 3),
    ("rs", 0, 1, 1),
    ("rs", 0, 0, 1),
    ("zt", 2),
    ("fin", 2),
    ("fin", 1),
    ("fin", 0),
)


def kernel(
    tok_in, routes_in, gates_in, wg, wu, wd, out,
    tok, shares, routes, gates, arrived, gate_w, up_w, down_w, hot, back_hot, weight, packed, rows, hidden, partial,
    leaving, coming, leaving_z, coming_z, summed, returned, mixed, owned,
    p1s, p1r, lw, ws, wr, p3s, p3r, ags, agr, zcs, zcr, rss, rsr, zss, zsr, rts, rtr, fs, fr,
):
    groups, ag, rs, order = GROUPS, GATHER, SCATTER, ORDER
    z = lax.axis_index("exp")
    t = lax.axis_index("tp")
    y = t // NC
    c = lax.rem(t, NC)
    home_core = lax.rem(z, NC)
    side = lax.rem(z + c, NC)
    is_home = side == 0
    turn = 2 * home_core - 1
    share = rows.shape[-1]

    def at(zz, yy, cc):
        return {"exp": zz, "tp": yy * NC + cc}

    def ring(v, n):
        return lax.rem(v + n, n)

    def send(src, dst, ssem, rsem, device):
        pltpu.make_async_remote_copy(
            src_ref=src, dst_ref=dst, send_sem=ssem, recv_sem=rsem, device_id=device, device_id_type=MESH
        ).start()

    def wait(ref, sem):
        pltpu.make_async_copy(ref, ref, sem).wait()

    def chunk(ref, index):
        return ref.at[:, pl.ds(pl.multiple_of(index * share, 128), share)]

    def center(j):
        return ring(y + j // 2 * (NY // 2), NY)

    def near(j, way, d):
        return ring(center(j) + (1 - 2 * way) * d, NY)

    partner = z - turn
    weights = ((wg, gate_w), (wu, up_w), (wd, down_w))
    small = ((tok_in, tok), (routes_in, routes), (gates_in, gates))
    for i, (src, dst) in enumerate(small):
        pltpu.make_async_copy(src, dst, lw.at[3 + i]).start()
    barrier = pltpu.get_barrier_semaphore()
    for dy in (4, 3, 5, 2, 6, 1, 7, 0):
        for dc in range(NC):
            if dy or dc:
                pl.semaphore_signal(
                    barrier, inc=1, device_id=at(z, ring(y + dy, NY), ring(c + dc, NC)), device_id_type=MESH
                )
    for dz in (4, 3, 5, 2, 6, 1, 7):
        pl.semaphore_signal(barrier, inc=1, device_id=at(ring(z + dz, NZ), y, c), device_id_type=MESH)
    for i, (src, dst) in enumerate(weights):
        pltpu.make_async_copy(src.at[0], dst.at[c], lw.at[i]).start()
    wait(tok, lw.at[3])
    pl.semaphore_wait(barrier, NY * NC - 1 + NZ - 1)

    for f in range(NY):
        g = (f + NY // 2) % NY
        shares[f, :, :share] = tok[:, f * share:(f + 1) * share]
        shares[f, :, share:] = tok[:, g * share:(g + 1) * share]

    for dy in (4, 3, 5, 2, 6, 1, 7):
        to = ring(y + dy, NY)
        send(shares.at[to], arrived.at[t], p1s.at[dy], p1r, at(z, to, home_core))

    @pl.when(is_home)
    def _():
        pltpu.make_async_copy(shares.at[y], arrived.at[t], p1r).start()

    @pl.when(jnp.logical_not(is_home))
    def _():
        send(shares.at[y], arrived.at[t], p1s.at[0], p1r, at(z, y, home_core))

    for i, (src, dst) in enumerate(weights):
        send(src.at[0], dst.at[c], ws.at[i], wr.at[i], at(z, y, 1 - c))

    for i, (src, dst) in enumerate(small[1:]):
        wait(dst, lw.at[4 + i])

    def pick(e, first, second):
        here = [jnp.broadcast_to(routes[k:k + 1, :], (ROWS, ROWS)) == e for k in range(2)]
        return jnp.where(here[0], first, 0.0) + jnp.where(here[1], second, 0.0)

    @pl.when(is_home)
    def _():
        row_ids = lax.broadcasted_iota(jnp.int32, (ROWS, ROWS), 0)
        col_ids = lax.broadcasted_iota(jnp.int32, (ROWS, ROWS), 1)
        earlier = jnp.where(row_ids < col_ids, 1.0, 0.0).astype(jnp.bfloat16)
        slots = row_ids.astype(jnp.float32)
        for e in range(EXPERTS):
            mine = pick(e, 1.0, 1.0)
            before = jnp.dot(mine.astype(jnp.bfloat16), earlier, preferred_element_type=jnp.float32)
            placed = jnp.where(before == slots, mine, 0.0)
            hot[e] = placed.astype(jnp.bfloat16)
        wait(arrived, p1r)
        block = arrived[...].astype(jnp.float32).reshape(ROWS, 2 * share).astype(jnp.bfloat16)
        for j, k in ((0, 0), (0, 1), (2, 1), (3, 0), (3, 1), (2, 0), (1, 1), (1, 0)):
            to = ring(z - turn * OFFSETS[0][j], NZ) if k == 0 else ring(z + turn * OFFSETS[1][j], NZ)
            e, lo = to // (NZ // EXPERTS), j // 2 * share
            slot = k * BLOCKS + j
            packed[slot] = jnp.dot(
                hot[e, :CAP, :], block[:, lo:lo + share], preferred_element_type=jnp.float32
            ).astype(jnp.bfloat16)
            if slot == 0:
                pltpu.make_async_copy(packed.at[slot], rows.at[j, center(j)], p3r.at[j]).start()
            else:
                send(packed.at[slot], rows.at[j, center(j)], p3s.at[slot], p3r.at[j], at(to, y, c))

    waited = set()

    def need(kind, j, *where):
        key = (kind, j) + where
        if key in waited:
            return
        waited.add(key)
        if kind == "p3":
            wait(rows.at[j, center(j)], p3r.at[j])
        elif kind == "ag":
            way, d = where
            wait(rows.at[j, near(j, way, -d)], agr.at[j, way, d - 1])
        elif kind == "zc":
            wait(rows.at[j, center(j ^ 2)], zcr.at[j, 0])
        elif kind == "zf":
            wait(rows.at[j, near(j ^ 2, HEAVY[j], -1)], zcr.at[j, 1])
        elif kind == "rs":
            way, d = where
            wait(coming.at[j, way, d - 1], rsr.at[j, way, d - 1])
        else:
            wait(coming_z.at[j, where[0]], zsr.at[j, where[0]])

    def gather(j, way, d):
        parent = ag[j][way][d - 1]
        piece = rows.at[j, near(j, way, -parent)]
        need("ag", j, way, parent) if parent else need("p3", j)
        to = ring(y + (1 - 2 * way) * (d - parent), NY)
        send(piece, piece, ags.at[j, way, d - 1], agr.at[j, way, d - 1], at(z, to, c))

    def share_center(j):
        need("p3", j)
        f = center(j)
        send(rows.at[j, f], rows.at[j ^ 2, f], zcs.at[j, 0], zcr.at[j ^ 2, 0], at(partner, y, c))

    def share_next(j):
        need("ag", j, HEAVY[j], 1)
        f = near(j, HEAVY[j], -1)
        send(rows.at[j, f], rows.at[j ^ 2, f], zcs.at[j, 1], zcr.at[j ^ 2, 1], at(partner, y, c))

    def up(g, core):
        if core == 0:
            for j in groups[g]:
                need("p3", j)
                for way in range(2):
                    for d in range(1, len(ag[j][way]) + 1):
                        need("ag", j, way, d)
                need("zc", j)
                need("zf", j)
        if "up" not in waited:
            waited.add("up")
            for i, (src, dst) in enumerate(weights[:2]):
                wait(dst.at[c], lw.at[i])
                wait(dst.at[1 - c], wr.at[i])
        x = jnp.concatenate(
            [jnp.concatenate([rows[j, f] for f in range(NY)], axis=1) for j in groups[g]], axis=0
        )
        gp = jnp.dot(x, gate_w[core], preferred_element_type=jnp.float32)
        u = jnp.dot(x, up_w[core], preferred_element_type=jnp.float32)
        n = gp.shape[1]
        hid = (gp / (1.0 + jnp.exp(-gp)) * u).astype(jnp.bfloat16)
        for i, j in enumerate(groups[g]):
            hidden[j, :, core * n:(core + 1) * n] = hid[i * CAP:(i + 1) * CAP]

    def down(g, half):
        if "down" not in waited:
            waited.add("down")
            wait(down_w.at[c], lw.at[2])
            wait(down_w.at[1 - c], wr.at[2])
        n = down_w.shape[1]
        h = jnp.concatenate([hidden[j] for j in groups[g]], axis=0)
        for f in range(half * NY // 2, (half + 1) * NY // 2, 2):
            lo, hi = f * share, (f + 2) * share
            r = jnp.dot(h[:, :n], down_w[0, :, lo:hi], preferred_element_type=jnp.float32)
            r += jnp.dot(h[:, n:], down_w[1, :, lo:hi], preferred_element_type=jnp.float32)
            for i, j in enumerate(groups[g]):
                partial[j, f] = r[i * CAP:(i + 1) * CAP, :share]
                partial[j, f + 1] = r[i * CAP:(i + 1) * CAP, share:]

    def across(j, i):
        f = center(j ^ 2) if i else near(j ^ 2, HEAVY[j], 1)
        leaving_z[j, i] = partial[j, f].astype(jnp.bfloat16)
        send(leaving_z.at[j, i], coming_z.at[j ^ 2, i], zss.at[j, i], zsr.at[j ^ 2, i], at(partner, y, c))

    def scatter(j, way, d):
        total = partial[j, near(j, way, d)]
        if (way, d) == (HEAVY[j], 1):
            need("zs", j, 0)
            total = total + coming_z[j, 0].astype(jnp.float32)
        total = total + children(j, way, d)
        leaving[j, way, d - 1] = total.astype(jnp.bfloat16)
        to = ring(y + (1 - 2 * way) * (d - rs[j][way][d - 1]), NY)
        send(
            leaving.at[j, way, d - 1], coming.at[j, way, d - 1], rss.at[j, way, d - 1], rsr.at[j, way, d - 1],
            at(z, to, c),
        )

    def children(j, way, d):
        total = 0.0
        for e, parent in enumerate(rs[j][way], 1):
            if parent == d:
                need("rs", j, way, e)
                total = total + coming[j, way, e - 1].astype(jnp.float32)
        return total

    def finish(j):
        need("zs", j, 1)
        total = partial[j, center(j)] + coming_z[j, 1].astype(jnp.float32)
        for way in range(2):
            total = total + children(j, way, 0)
        summed[j] = total.astype(jnp.bfloat16)
        back = ring(z + turn * (OFFSETS[0][j] + side * (OFFSETS[1][j] - OFFSETS[0][j])), NZ)
        if j == 0:
            @pl.when(is_home)
            def _():
                pltpu.make_async_copy(summed.at[j], returned.at[z], rtr.at[z]).start()

            @pl.when(jnp.logical_not(is_home))
            def _():
                send(summed.at[j], returned.at[z], rts.at[j], rtr.at[z], at(back, y, c))
        else:
            send(summed.at[j], returned.at[z], rts.at[j], rtr.at[z], at(back, y, c))

    def prepare():
        @pl.when(is_home)
        def _():
            row_ids = lax.broadcasted_iota(jnp.int32, (ROWS, ROWS), 0)
            col_ids = lax.broadcasted_iota(jnp.int32, (ROWS, ROWS), 1)
            g0, g1 = (jnp.broadcast_to(gates[k:k + 1, :], (ROWS, ROWS)) for k in range(2))
            for e in range(EXPERTS):
                back_hot[e] = hot[e].astype(jnp.float32).T.astype(jnp.bfloat16)
                gate = jnp.sum(jnp.where(row_ids == col_ids, pick(e, g0, g1), 0.0), axis=1, keepdims=True)
                weight[e] = jnp.broadcast_to(gate, (ROWS, 128))

    def across_next(j):
        across(j, 0)

    def across_center(j):
        across(j, 1)

    step = {"zs": across_next, "zt": across_center, "prep": prepare, "ag": gather, "zc": share_center, "zf": share_next, "up": up, "down": down, "rs": scatter, "fin": finish}
    for task in order:
        step[task[0]](*task[1:])

    @pl.when(is_home)
    def _():
        totals = [jnp.zeros((ROWS, share), jnp.float32)] * 2
        for j in [task[1] for task in order if task[0] == "fin"]:
            for k in range(2):
                to = ring(z - turn * OFFSETS[0][j], NZ) if k == 0 else ring(z + turn * OFFSETS[1][j], NZ)
                e = to // (NZ // EXPERTS)
                wait(returned.at[to], rtr.at[to])
                picked = jnp.dot(back_hot[e, :, :CAP], returned[to], preferred_element_type=jnp.float32)
                totals[j // 2] += jnp.concatenate([weight[e]] * (share // 128), axis=1) * picked
        for i in range(2):
            mixed[:, :, i * share:(i + 1) * share] = totals[i].reshape(
                NY * NC, ROWS // (NY * NC), share
            ).astype(jnp.bfloat16)
        for dy in (4, 3, 5, 2, 6, 1, 7, 0):
            for dc in range(NC):
                to, core = ring(y + dy, NY), ring(c + dc, NC)
                src = mixed.at[to * NC + core]
                if dy == 0 and dc == 0:
                    pltpu.make_async_copy(src, owned.at[y], fr).start()
                else:
                    send(src, owned.at[y], fs.at[dy * NC + dc], fr, at(z, to, core))

    for dy in range(1, NY):
        wait(shares.at[0], p1s.at[dy])
    for i, (src, dst) in enumerate(weights):
        wait(src.at[0], ws.at[i])
    for j in range(BLOCKS):
        for way in range(2):
            for h in range(len(ag[j][way])):
                wait(rows.at[j, 0], ags.at[j, way, h])
            for h in range(len(rs[j][way])):
                wait(leaving.at[j, way, h], rss.at[j, way, h])
        for i in range(2):
            wait(rows.at[j, 0], zcs.at[j, i])
            wait(leaving_z.at[j, i], zss.at[j, i])
        if j > 0:
            wait(summed.at[j], rts.at[j])

    @pl.when(is_home)
    def _():
        for i in range(1, 2 * BLOCKS):
            wait(packed.at[0], p3s.at[i])
        for i in range(1, NY * NC):
            wait(mixed.at[0], fs.at[i])

    @pl.when(jnp.logical_not(is_home))
    def _():
        wait(shares.at[0], p1s.at[0])
        wait(summed.at[0], rts.at[0])

    wait(owned, fr)
    for f in range(NY):
        both = owned[f, :, :share].astype(jnp.float32)
        both += owned[(f + NY // 2) % NY, :, share:].astype(jnp.float32)
        out[:, f * share:(f + 1) * share] = both.astype(jnp.bfloat16)


def local(tokens, routes, gates, w_gate, w_up, w_down):
    tok_dev, width = tokens.shape
    hid = w_gate.shape[2]
    share = width // NY
    bf16, f32 = jnp.bfloat16, jnp.float32
    dma = pltpu.SemaphoreType.DMA
    hbm = pl.BlockSpec(memory_space=pltpu.HBM)
    return pl.pallas_call(
        kernel,
        out_shape=jax.ShapeDtypeStruct((tok_dev, width), bf16),
        in_specs=[hbm] * 6,
        out_specs=pl.BlockSpec(memory_space=pltpu.VMEM),
        scratch_shapes=[
            pltpu.VMEM((tok_dev, width), bf16),
            pltpu.VMEM((NY, tok_dev, 2 * share), bf16),
            pltpu.VMEM((2, ROWS), jnp.int32),
            pltpu.VMEM((2, ROWS), f32),
            pltpu.VMEM((NY * NC, tok_dev, 2 * share), bf16),
            pltpu.VMEM((NC, width, hid), bf16),
            pltpu.VMEM((NC, width, hid), bf16),
            pltpu.VMEM((NC, hid, width), bf16),
            pltpu.VMEM((EXPERTS, ROWS, ROWS), bf16),
            pltpu.VMEM((EXPERTS, ROWS, ROWS), bf16),
            pltpu.VMEM((EXPERTS, ROWS, 128), f32),
            pltpu.VMEM((2 * BLOCKS, CAP, share), bf16),
            pltpu.VMEM((BLOCKS, NY, CAP, share), bf16),
            pltpu.VMEM((BLOCKS, CAP, NC * hid), bf16),
            pltpu.VMEM((BLOCKS, NY, CAP, share), f32),
            pltpu.VMEM((BLOCKS, 2, 3, CAP, share), bf16),
            pltpu.VMEM((BLOCKS, 2, 3, CAP, share), bf16),
            pltpu.VMEM((BLOCKS, 2, CAP, share), bf16),
            pltpu.VMEM((BLOCKS, 2, CAP, share), bf16),
            pltpu.VMEM((BLOCKS, CAP, share), bf16),
            pltpu.VMEM((NZ, CAP, share), bf16),
            pltpu.VMEM((NY * NC, tok_dev, 2 * share), bf16),
            pltpu.VMEM((NY, tok_dev, 2 * share), bf16),
            dma((NY,)), dma,
            dma((6,)), dma((3,)), dma((3,)),
            dma((2 * BLOCKS,)), dma((BLOCKS,)),
            dma((BLOCKS, 2, 3)), dma((BLOCKS, 2, 3)),
            dma((BLOCKS, 2)), dma((BLOCKS, 2)),
            dma((BLOCKS, 2, 3)), dma((BLOCKS, 2, 3)),
            dma((BLOCKS, 2)), dma((BLOCKS, 2)),
            dma((BLOCKS,)), dma((NZ,)),
            dma((NY * NC,)), dma,
        ],
        compiler_params=pltpu.CompilerParams(
            collective_id=0, has_side_effects=True, vmem_limit_bytes=62 * 2**20
        ),
        name="moe",
    )(tokens, routes.T, gates.T, w_gate, w_up, w_down)


def solution(mesh):
    return jax.shard_map(
        local,
        mesh=mesh,
        in_specs=(
            P(("dp", "exp", "tp"), None),
            P(("dp", "exp"), None),
            P(("dp", "exp"), None),
            P("exp", None, "tp"),
            P("exp", None, "tp"),
            P("exp", "tp", None),
        ),
        out_specs=P(("dp", "exp", "tp"), None),
        check_vma=False,
    )
```

```python
import jax
import jax.numpy as jnp
from jax import lax
from jax.experimental import pallas as pl
from jax.experimental.pallas import tpu as pltpu
from jax.sharding import PartitionSpec as P

MESH = pl.DeviceIdType.MESH
EXPERTS = 4
NZ = 8
NY = 8
NC = 2
ROWS = 128
CAP = 80
BLOCKS = NZ // NC
OFFSETS = ((0, 2, -2, 4), (1, 3, -1, -3))


HEAVY = (0, 1, 0, 1)


GROUPS = ((0, 2), (1, 3))
GATHER = (((0, 1, 2), (0, 1)), ((0, 1), (0, 1, 2)), ((0, 1, 2), (0, 1)), ((0, 1), (0, 1, 2)))
SCATTER = (((0, 1, 2), (0, 1)), ((0, 1), (0, 1)), ((0, 1, 2), (0, 1)), ((0, 1), (0, 1)))
ORDER = (
    ("ag", 0, 0, 1),
    ("ag", 0, 1, 1),
    ("prep",),
    ("zc", 0),
    ("ag", 2, 0, 1),
    ("ag", 2, 1, 1),
    ("zc", 2),
    ("ag", 0, 0, 2),
    ("ag", 1, 1, 1),
    ("ag", 1, 0, 1),
    ("ag", 3, 1, 1),
    ("ag", 2, 0, 2),
    ("ag", 0, 1, 2),
    ("ag", 0, 0, 3),
    ("zf", 2),
    ("zf", 0),
    ("ag", 1, 1, 2),
    ("ag", 3, 0, 1),
    ("zc", 1),
    ("ag", 2, 1, 2),
    ("ag", 2, 0, 3),
    ("zc", 3),
    ("ag", 1, 0, 2),
    ("zf", 1),
    ("ag", 3, 1, 2),
    ("ag", 1, 1, 3),
    ("zf", 3),
    ("up", 0, 0),
    ("ag", 3, 0, 2),
    ("ag", 3, 1, 3),
    ("up", 0, 1),
    ("down", 0, 0),
    ("down", 0, 1),
    ("zt", 0),
    ("rs", 0, 1, 2),
    ("rs", 2, 1, 2),
    ("rs", 2, 0, 3),
    ("zs", 2),
    ("zs", 0),
    ("rs", 0, 0, 3),
    ("up", 1, 0),
    ("up", 1, 1),
    ("down", 1, 0),
    ("down", 1, 1),
    ("rs", 1, 0, 2),
    ("zu", 3),
    ("rs", 2, 0, 2),
    ("zs", 1),
    ("rs", 3, 0, 2),
    ("rs", 3, 1, 2),
    ("zu", 1),
    ("rs", 0, 1, 1),
    ("zs", 3),
    ("rs", 0, 0, 2),
    ("rs", 1, 1, 2),
    ("rs", 2, 1, 1),
    ("zt", 1),
    ("rs", 2, 0, 1),
    ("rs", 3, 1, 1),
    ("rs", 3, 0, 1),
    ("zt", 3),
    ("rs", 1, 0, 1),
    ("rs", 1, 1, 1),
    ("rs", 0, 0, 1),
    ("zt", 2),
    ("fin", 2),
    ("fin", 3),
    ("fin", 1),
    ("fin", 0),
)


def kernel(
    tok_in, routes_in, gates_in, wg, wu, wd, out,
    tok, shares, routes, gates, arrived, gate_w, up_w, down_w, hot, back_hot, weight, packed, rows, hidden, partial,
    leaving, coming, leaving_z, coming_z, summed, returned, mixed, owned,
    p1s, p1r, lw, ws, wr, p3s, p3r, ags, agr, zcs, zcr, rss, rsr, zss, zsr, rts, rtr, fs, fr,
):
    groups, ag, rs, order = GROUPS, GATHER, SCATTER, ORDER
    z = lax.axis_index("exp")
    t = lax.axis_index("tp")
    y = t // NC
    c = lax.rem(t, NC)
    home_core = lax.rem(z, NC)
    side = lax.rem(z + c, NC)
    is_home = side == 0
    turn = 2 * home_core - 1
    share = rows.shape[-1]

    def at(zz, yy, cc):
        return {"exp": zz, "tp": yy * NC + cc}

    def ring(v, n):
        return lax.rem(v + n, n)

    def send(src, dst, ssem, rsem, device):
        pltpu.make_async_remote_copy(
            src_ref=src, dst_ref=dst, send_sem=ssem, recv_sem=rsem, device_id=device, device_id_type=MESH
        ).start()

    def wait(ref, sem):
        pltpu.make_async_copy(ref, ref, sem).wait()

    def chunk(ref, index):
        return ref.at[:, pl.ds(pl.multiple_of(index * share, 128), share)]

    def center(j):
        return ring(y + j // 2 * (NY // 2), NY)

    def near(j, way, d):
        return ring(center(j) + (1 - 2 * way) * d, NY)

    partner = z - turn
    weights = ((wg, gate_w), (wu, up_w), (wd, down_w))
    small = ((tok_in, tok), (routes_in, routes), (gates_in, gates))
    for i, (src, dst) in enumerate(small):
        pltpu.make_async_copy(src, dst, lw.at[3 + i]).start()
    barrier = pltpu.get_barrier_semaphore()
    for dy in (4, 3, 5, 2, 6, 1, 7, 0):
        for dc in range(NC):
            if dy or dc:
                pl.semaphore_signal(
                    barrier, inc=1, device_id=at(z, ring(y + dy, NY), ring(c + dc, NC)), device_id_type=MESH
                )
    for dz in (4, 3, 5, 2, 6, 1, 7):
        pl.semaphore_signal(barrier, inc=1, device_id=at(ring(z + dz, NZ), y, c), device_id_type=MESH)
    for i, (src, dst) in enumerate(weights):
        pltpu.make_async_copy(src.at[0], dst.at[c], lw.at[i]).start()
    wait(tok, lw.at[3])
    pl.semaphore_wait(barrier, NY * NC - 1 + NZ - 1)

    for f in range(NY):
        g = (f + NY // 2) % NY
        shares[f, :, :share] = tok[:, f * share:(f + 1) * share]
        shares[f, :, share:] = tok[:, g * share:(g + 1) * share]

    for dy in (4, 3, 5, 2, 6, 1, 7):
        to = ring(y + dy, NY)
        send(shares.at[to], arrived.at[t], p1s.at[dy], p1r, at(z, to, home_core))

    @pl.when(is_home)
    def _():
        pltpu.make_async_copy(shares.at[y], arrived.at[t], p1r).start()

    @pl.when(jnp.logical_not(is_home))
    def _():
        send(shares.at[y], arrived.at[t], p1s.at[0], p1r, at(z, y, home_core))

    for i, (src, dst) in enumerate(weights):
        send(src.at[0], dst.at[c], ws.at[i], wr.at[i], at(z, y, 1 - c))

    for i, (src, dst) in enumerate(small[1:]):
        wait(dst, lw.at[4 + i])

    def pick(e, first, second):
        here = [jnp.broadcast_to(routes[k:k + 1, :], (ROWS, ROWS)) == e for k in range(2)]
        return jnp.where(here[0], first, 0.0) + jnp.where(here[1], second, 0.0)

    @pl.when(is_home)
    def _():
        row_ids = lax.broadcasted_iota(jnp.int32, (ROWS, ROWS), 0)
        col_ids = lax.broadcasted_iota(jnp.int32, (ROWS, ROWS), 1)
        earlier = jnp.where(row_ids < col_ids, 1.0, 0.0).astype(jnp.bfloat16)
        slots = row_ids.astype(jnp.float32)
        for e in range(EXPERTS):
            mine = pick(e, 1.0, 1.0)
            before = jnp.dot(mine.astype(jnp.bfloat16), earlier, preferred_element_type=jnp.float32)
            placed = jnp.where(before == slots, mine, 0.0)
            hot[e] = placed.astype(jnp.bfloat16)
        wait(arrived, p1r)
        block = arrived[...].astype(jnp.float32).reshape(ROWS, 2 * share).astype(jnp.bfloat16)
        for j, k in ((0, 0), (0, 1), (2, 1), (3, 0), (3, 1), (2, 0), (1, 1), (1, 0)):
            to = ring(z - turn * OFFSETS[0][j], NZ) if k == 0 else ring(z + turn * OFFSETS[1][j], NZ)
            e, lo = to // (NZ // EXPERTS), j // 2 * share
            slot = k * BLOCKS + j
            packed[slot] = jnp.dot(
                hot[e, :CAP, :], block[:, lo:lo + share], preferred_element_type=jnp.float32
            ).astype(jnp.bfloat16)
            if slot == 0:
                pltpu.make_async_copy(packed.at[slot], rows.at[j, center(j)], p3r.at[j]).start()
            else:
                send(packed.at[slot], rows.at[j, center(j)], p3s.at[slot], p3r.at[j], at(to, y, c))

    def short(rings, j, way):
        return len(rings[j][way]) == 2

    waited = set()

    def need(kind, j, *where):
        key = (kind, j) + where
        if key in waited:
            return
        waited.add(key)
        if kind == "p3":
            wait(rows.at[j, center(j)], p3r.at[j])
        elif kind == "ag":
            way, d = where
            wait(rows.at[j, near(j, way, -d)], agr.at[j, way, d - 1])
        elif kind == "zc":
            wait(rows.at[j, center(j ^ 2)], zcr.at[j, 0])
        elif kind == "zf":
            wait(rows.at[j, near(j ^ 2, HEAVY[j], -1)], zcr.at[j, 1])
        elif kind == "zg":
            wait(rows.at[j, near(j ^ 2, 1 - HEAVY[j], -1)], zcr.at[j, 2])
        elif kind == "rs":
            way, d = where
            wait(coming.at[j, way, d - 1], rsr.at[j, way, d - 1])
        else:
            wait(coming_z.at[j, where[0]], zsr.at[j, where[0]])

    def gather(j, way, d):
        parent = ag[j][way][d - 1]
        piece = rows.at[j, near(j, way, -parent)]
        need("ag", j, way, parent) if parent else need("p3", j)
        to = ring(y + (1 - 2 * way) * (d - parent), NY)
        send(piece, piece, ags.at[j, way, d - 1], agr.at[j, way, d - 1], at(z, to, c))

    def share_center(j):
        need("p3", j)
        f = center(j)
        send(rows.at[j, f], rows.at[j ^ 2, f], zcs.at[j, 0], zcr.at[j ^ 2, 0], at(partner, y, c))

    def share_near(j, way, i):
        need("ag", j, way, 1)
        f = near(j, way, -1)
        send(rows.at[j, f], rows.at[j ^ 2, f], zcs.at[j, i], zcr.at[j ^ 2, i], at(partner, y, c))

    def up(g, core):
        if core == 0:
            for j in groups[g]:
                need("p3", j)
                for way in range(2):
                    for d in range(1, len(ag[j][way]) + 1):
                        need("ag", j, way, d)
                need("zc", j)
                if short(ag, j, 1 - HEAVY[j]):
                    need("zf", j)
                if short(ag, j, HEAVY[j]):
                    need("zg", j)
        if "up" not in waited:
            waited.add("up")
            for i, (src, dst) in enumerate(weights[:2]):
                wait(dst.at[c], lw.at[i])
                wait(dst.at[1 - c], wr.at[i])
        x = jnp.concatenate(
            [jnp.concatenate([rows[j, f] for f in range(NY)], axis=1) for j in groups[g]], axis=0
        )
        gp = jnp.dot(x, gate_w[core], preferred_element_type=jnp.float32)
        u = jnp.dot(x, up_w[core], preferred_element_type=jnp.float32)
        n = gp.shape[1]
        hid = (gp / (1.0 + jnp.exp(-gp)) * u).astype(jnp.bfloat16)
        for i, j in enumerate(groups[g]):
            hidden[j, :, core * n:(core + 1) * n] = hid[i * CAP:(i + 1) * CAP]

    def down(g, half):
        if "down" not in waited:
            waited.add("down")
            wait(down_w.at[c], lw.at[2])
            wait(down_w.at[1 - c], wr.at[2])
        n = down_w.shape[1]
        h = jnp.concatenate([hidden[j] for j in groups[g]], axis=0)
        for f in range(half * NY // 2, (half + 1) * NY // 2, 2):
            lo, hi = f * share, (f + 2) * share
            r = jnp.dot(h[:, :n], down_w[0, :, lo:hi], preferred_element_type=jnp.float32)
            r += jnp.dot(h[:, n:], down_w[1, :, lo:hi], preferred_element_type=jnp.float32)
            for i, j in enumerate(groups[g]):
                partial[j, f] = r[i * CAP:(i + 1) * CAP, :share]
                partial[j, f + 1] = r[i * CAP:(i + 1) * CAP, share:]

    def across(j, i):
        f = center(j ^ 2) if i == 1 else near(j ^ 2, HEAVY[j] if i == 0 else 1 - HEAVY[j], 1)
        leaving_z[j, i] = partial[j, f].astype(jnp.bfloat16)
        send(leaving_z.at[j, i], coming_z.at[j ^ 2, i], zss.at[j, i], zsr.at[j ^ 2, i], at(partner, y, c))

    def scatter(j, way, d):
        total = partial[j, near(j, way, d)]
        if d == 1 and short(rs, j, 1 - way):
            i = 0 if way == HEAVY[j] else 2
            need("zs", j, i)
            total = total + coming_z[j, i].astype(jnp.float32)
        total = total + children(j, way, d)
        leaving[j, way, d - 1] = total.astype(jnp.bfloat16)
        to = ring(y + (1 - 2 * way) * (d - rs[j][way][d - 1]), NY)
        send(
            leaving.at[j, way, d - 1], coming.at[j, way, d - 1], rss.at[j, way, d - 1], rsr.at[j, way, d - 1],
            at(z, to, c),
        )

    def children(j, way, d):
        total = 0.0
        for e, parent in enumerate(rs[j][way], 1):
            if parent == d:
                need("rs", j, way, e)
                total = total + coming[j, way, e - 1].astype(jnp.float32)
        return total

    def finish(j):
        need("zs", j, 1)
        total = partial[j, center(j)] + coming_z[j, 1].astype(jnp.float32)
        for way in range(2):
            total = total + children(j, way, 0)
        summed[j] = total.astype(jnp.bfloat16)
        back = ring(z + turn * (OFFSETS[0][j] + side * (OFFSETS[1][j] - OFFSETS[0][j])), NZ)
        if j == 0:
            @pl.when(is_home)
            def _():
                pltpu.make_async_copy(summed.at[j], returned.at[z], rtr.at[z]).start()

            @pl.when(jnp.logical_not(is_home))
            def _():
                send(summed.at[j], returned.at[z], rts.at[j], rtr.at[z], at(back, y, c))
        else:
            send(summed.at[j], returned.at[z], rts.at[j], rtr.at[z], at(back, y, c))

    def prepare():
        @pl.when(is_home)
        def _():
            row_ids = lax.broadcasted_iota(jnp.int32, (ROWS, ROWS), 0)
            col_ids = lax.broadcasted_iota(jnp.int32, (ROWS, ROWS), 1)
            g0, g1 = (jnp.broadcast_to(gates[k:k + 1, :], (ROWS, ROWS)) for k in range(2))
            for e in range(EXPERTS):
                back_hot[e] = hot[e].astype(jnp.float32).T.astype(jnp.bfloat16)
                gate = jnp.sum(jnp.where(row_ids == col_ids, pick(e, g0, g1), 0.0), axis=1, keepdims=True)
                weight[e] = jnp.broadcast_to(gate, (ROWS, 128))

    step = {
        "zf": lambda j: share_near(j, HEAVY[j], 1), "zg": lambda j: share_near(j, 1 - HEAVY[j], 2),
        "zs": lambda j: across(j, 0), "zt": lambda j: across(j, 1), "zu": lambda j: across(j, 2), "prep": prepare,
        "ag": gather, "zc": share_center, "up": up, "down": down, "rs": scatter, "fin": finish}
    for task in order:
        step[task[0]](*task[1:])

    @pl.when(is_home)
    def _():
        totals = [jnp.zeros((ROWS, share), jnp.float32)] * 2
        for j in [task[1] for task in order if task[0] == "fin"]:
            for k in range(2):
                to = ring(z - turn * OFFSETS[0][j], NZ) if k == 0 else ring(z + turn * OFFSETS[1][j], NZ)
                e = to // (NZ // EXPERTS)
                wait(returned.at[to], rtr.at[to])
                picked = jnp.dot(back_hot[e, :, :CAP], returned[to], preferred_element_type=jnp.float32)
                totals[j // 2] += jnp.concatenate([weight[e]] * (share // 128), axis=1) * picked
        for i in range(2):
            mixed[:, :, i * share:(i + 1) * share] = totals[i].reshape(
                NY * NC, ROWS // (NY * NC), share
            ).astype(jnp.bfloat16)
        for dy in (4, 3, 5, 2, 6, 1, 7, 0):
            for dc in range(NC):
                to, core = ring(y + dy, NY), ring(c + dc, NC)
                src = mixed.at[to * NC + core]
                if dy == 0 and dc == 0:
                    pltpu.make_async_copy(src, owned.at[y], fr).start()
                else:
                    send(src, owned.at[y], fs.at[dy * NC + dc], fr, at(z, to, core))

    for dy in range(1, NY):
        wait(shares.at[0], p1s.at[dy])
    for i, (src, dst) in enumerate(weights):
        wait(src.at[0], ws.at[i])
    for j in range(BLOCKS):
        for way in range(2):
            for h in range(len(ag[j][way])):
                wait(rows.at[j, 0], ags.at[j, way, h])
            for h in range(len(rs[j][way])):
                wait(leaving.at[j, way, h], rss.at[j, way, h])
        for i, way in enumerate((None, 1 - HEAVY[j], HEAVY[j])):
            if way is None or short(ag, j, way):
                wait(rows.at[j, 0], zcs.at[j, i])
        for i, way in enumerate((1 - HEAVY[j], None, HEAVY[j])):
            if way is None or short(rs, j, way):
                wait(leaving_z.at[j, i], zss.at[j, i])
        if j > 0:
            wait(summed.at[j], rts.at[j])

    @pl.when(is_home)
    def _():
        for i in range(1, 2 * BLOCKS):
            wait(packed.at[0], p3s.at[i])
        for i in range(1, NY * NC):
            wait(mixed.at[0], fs.at[i])

    @pl.when(jnp.logical_not(is_home))
    def _():
        wait(shares.at[0], p1s.at[0])
        wait(summed.at[0], rts.at[0])

    wait(owned, fr)
    for f in range(NY):
        both = owned[f, :, :share].astype(jnp.float32)
        both += owned[(f + NY // 2) % NY, :, share:].astype(jnp.float32)
        out[:, f * share:(f + 1) * share] = both.astype(jnp.bfloat16)


def local(tokens, routes, gates, w_gate, w_up, w_down):
    tok_dev, width = tokens.shape
    hid = w_gate.shape[2]
    share = width // NY
    bf16, f32 = jnp.bfloat16, jnp.float32
    dma = pltpu.SemaphoreType.DMA
    hbm = pl.BlockSpec(memory_space=pltpu.HBM)
    return pl.pallas_call(
        kernel,
        out_shape=jax.ShapeDtypeStruct((tok_dev, width), bf16),
        in_specs=[hbm] * 6,
        out_specs=pl.BlockSpec(memory_space=pltpu.VMEM),
        scratch_shapes=[
            pltpu.VMEM((tok_dev, width), bf16),
            pltpu.VMEM((NY, tok_dev, 2 * share), bf16),
            pltpu.VMEM((2, ROWS), jnp.int32),
            pltpu.VMEM((2, ROWS), f32),
            pltpu.VMEM((NY * NC, tok_dev, 2 * share), bf16),
            pltpu.VMEM((NC, width, hid), bf16),
            pltpu.VMEM((NC, width, hid), bf16),
            pltpu.VMEM((NC, hid, width), bf16),
            pltpu.VMEM((EXPERTS, ROWS, ROWS), bf16),
            pltpu.VMEM((EXPERTS, ROWS, ROWS), bf16),
            pltpu.VMEM((EXPERTS, ROWS, 128), f32),
            pltpu.VMEM((2 * BLOCKS, CAP, share), bf16),
            pltpu.VMEM((BLOCKS, NY, CAP, share), bf16),
            pltpu.VMEM((BLOCKS, CAP, NC * hid), bf16),
            pltpu.VMEM((BLOCKS, NY, CAP, share), f32),
            pltpu.VMEM((BLOCKS, 2, 3, CAP, share), bf16),
            pltpu.VMEM((BLOCKS, 2, 3, CAP, share), bf16),
            pltpu.VMEM((BLOCKS, 3, CAP, share), bf16),
            pltpu.VMEM((BLOCKS, 3, CAP, share), bf16),
            pltpu.VMEM((BLOCKS, CAP, share), bf16),
            pltpu.VMEM((NZ, CAP, share), bf16),
            pltpu.VMEM((NY * NC, tok_dev, 2 * share), bf16),
            pltpu.VMEM((NY, tok_dev, 2 * share), bf16),
            dma((NY,)), dma,
            dma((6,)), dma((3,)), dma((3,)),
            dma((2 * BLOCKS,)), dma((BLOCKS,)),
            dma((BLOCKS, 2, 3)), dma((BLOCKS, 2, 3)),
            dma((BLOCKS, 3)), dma((BLOCKS, 3)),
            dma((BLOCKS, 2, 3)), dma((BLOCKS, 2, 3)),
            dma((BLOCKS, 3)), dma((BLOCKS, 3)),
            dma((BLOCKS,)), dma((NZ,)),
            dma((NY * NC,)), dma,
        ],
        compiler_params=pltpu.CompilerParams(
            collective_id=0, has_side_effects=True, vmem_limit_bytes=62 * 2**20
        ),
        name="moe",
    )(tokens, routes.T, gates.T, w_gate, w_up, w_down)


def solution(mesh):
    return jax.shard_map(
        local,
        mesh=mesh,
        in_specs=(
            P(("dp", "exp", "tp"), None),
            P(("dp", "exp"), None),
            P(("dp", "exp"), None),
            P("exp", None, "tp"),
            P("exp", None, "tp"),
            P("exp", "tp", None),
        ),
        out_specs=P(("dp", "exp", "tp"), None),
        check_vma=False,
    )
```

```python
import jax
import jax.numpy as jnp
from jax import lax
from jax.experimental import pallas as pl
from jax.experimental.pallas import tpu as pltpu
from jax.sharding import PartitionSpec as P

MESH = pl.DeviceIdType.MESH
EXPERTS = 4
NZ = 8
NY = 8
NC = 2
ROWS = 128
CAP = 80
BLOCKS = NZ // NC
OFFSETS = ((0, 2, -2, 4), (1, 3, -1, -3))


HEAVY = (0, 1, 0, 1)


GROUPS = ((0, 2), (1, 3))
GATHER = (((0, 1, 2), (0, 1)), ((0, 1), (0, 1, 2)), ((0, 1, 2), (0, 1)), ((0, 1), (0, 1, 2)))
SCATTER = (((0, 1, 2), (0, 1)), ((0, 1), (0, 1)), ((0, 1, 2), (0, 1)), ((0, 1), (0, 1)))
ORDER = (
    ("ag", 0, 0, 1),
    ("ag", 0, 1, 1),
    ("prep",),
    ("zc", 0),
    ("ag", 2, 0, 1),
    ("ag", 2, 1, 1),
    ("zc", 2),
    ("ag", 0, 0, 2),
    ("ag", 1, 1, 1),
    ("ag", 1, 0, 1),
    ("ag", 3, 1, 1),
    ("ag", 2, 0, 2),
    ("ag", 0, 1, 2),
    ("ag", 0, 0, 3),
    ("zf", 2),
    ("zf", 0),
    ("ag", 1, 1, 2),
    ("ag", 3, 0, 1),
    ("zc", 1),
    ("ag", 2, 1, 2),
    ("ag", 2, 0, 3),
    ("zc", 3),
    ("ag", 1, 0, 2),
    ("zf", 1),
    ("ag", 3, 1, 2),
    ("ag", 1, 1, 3),
    ("zf", 3),
    ("up", 0, 0),
    ("ag", 3, 0, 2),
    ("ag", 3, 1, 3),
    ("up", 0, 1),
    ("down", 0, 0),
    ("down", 0, 1),
    ("zt", 0),
    ("rs", 0, 1, 2),
    ("rs", 2, 1, 2),
    ("rs", 2, 0, 3),
    ("zs", 2),
    ("zs", 0),
    ("rs", 0, 0, 3),
    ("up", 1, 0),
    ("up", 1, 1),
    ("down", 1, 0),
    ("down", 1, 1),
    ("rs", 1, 0, 2),
    ("zu", 3),
    ("rs", 2, 0, 2),
    ("zs", 1),
    ("rs", 3, 0, 2),
    ("rs", 3, 1, 2),
    ("zu", 1),
    ("rs", 0, 1, 1),
    ("zs", 3),
    ("rs", 0, 0, 2),
    ("rs", 1, 1, 2),
    ("rs", 2, 1, 1),
    ("zt", 1),
    ("rs", 2, 0, 1),
    ("rs", 3, 1, 1),
    ("rs", 3, 0, 1),
    ("zt", 3),
    ("rs", 1, 0, 1),
    ("rs", 1, 1, 1),
    ("rs", 0, 0, 1),
    ("zt", 2),
    ("fin", 2),
    ("fin", 3),
    ("fin", 1),
    ("fin", 0),
)


def kernel(
    tok_in, routes_in, gates_in, wg, wu, wd, out,
    tok, shares, routes, gates, arrived, gate_w, up_w, down_w, hot, back_hot, weight, packed, rows, hidden, partial,
    leaving, coming, leaving_z, coming_z, summed, returned, mixed, owned,
    p1s, p1r, lw, ws, wr, p3s, p3r, ags, agr, zcs, zcr, rss, rsr, zss, zsr, rts, rtr, fs, fr,
):
    groups, ag, rs, order = GROUPS, GATHER, SCATTER, ORDER
    z = lax.axis_index("exp")
    t = lax.axis_index("tp")
    y = t // NC
    c = lax.rem(t, NC)
    home_core = lax.rem(z, NC)
    side = lax.rem(z + c, NC)
    is_home = side == 0
    turn = 2 * home_core - 1
    share = rows.shape[-1]

    def at(zz, yy, cc):
        return {"exp": zz, "tp": yy * NC + cc}

    def ring(v, n):
        return lax.rem(v + n, n)

    def send(src, dst, ssem, rsem, device):
        pltpu.make_async_remote_copy(
            src_ref=src, dst_ref=dst, send_sem=ssem, recv_sem=rsem, device_id=device, device_id_type=MESH
        ).start()

    def wait(ref, sem):
        pltpu.make_async_copy(ref, ref, sem).wait()

    def chunk(ref, index):
        return ref.at[:, pl.ds(pl.multiple_of(index * share, 128), share)]

    def center(j):
        return ring(y + j // 2 * (NY // 2), NY)

    def near(j, way, d):
        return ring(center(j) + (1 - 2 * way) * d, NY)

    partner = z - turn
    weights = ((wg, gate_w), (wu, up_w), (wd, down_w))
    small = ((tok_in, tok), (routes_in, routes), (gates_in, gates))
    barrier = pltpu.get_barrier_semaphore()
    for d in (4, 3, 5, 2, 6, 1, 7, 0):
        peers = [at(z, ring(y + d, NY), c), at(z, ring(y + d, NY), 1 - c), at(ring(z + d, NZ), y, c)]
        for peer in peers if d else peers[1:2]:
            pl.semaphore_signal(barrier, inc=1, device_id=peer, device_id_type=MESH)
    for i, (src, dst) in enumerate(small):
        pltpu.make_async_copy(src, dst, lw.at[3 + i]).start()
    for i, (src, dst) in enumerate(weights):
        pltpu.make_async_copy(src.at[0], dst.at[c], lw.at[i]).start()
    wait(tok, lw.at[3])
    for f in range(NY):
        g = (f + NY // 2) % NY
        shares[f, :, :share] = tok[:, f * share:(f + 1) * share]
        shares[f, :, share:] = tok[:, g * share:(g + 1) * share]
    pl.semaphore_wait(barrier, NY * NC - 1 + NZ - 1)

    for dy in (4, 3, 5, 2, 6, 1, 7):
        to = ring(y + dy, NY)
        send(shares.at[to], arrived.at[t], p1s.at[dy], p1r, at(z, to, home_core))

    @pl.when(is_home)
    def _():
        pltpu.make_async_copy(shares.at[y], arrived.at[t], p1r).start()

    @pl.when(jnp.logical_not(is_home))
    def _():
        send(shares.at[y], arrived.at[t], p1s.at[0], p1r, at(z, y, home_core))

    for i, (src, dst) in enumerate(weights):
        send(src.at[0], dst.at[c], ws.at[i], wr.at[i], at(z, y, 1 - c))

    for i, (src, dst) in enumerate(small[1:]):
        wait(dst, lw.at[4 + i])

    def pick(e, first, second):
        here = [jnp.broadcast_to(routes[k:k + 1, :], (ROWS, ROWS)) == e for k in range(2)]
        return jnp.where(here[0], first, 0.0) + jnp.where(here[1], second, 0.0)

    @pl.when(is_home)
    def _():
        row_ids = lax.broadcasted_iota(jnp.int32, (ROWS, ROWS), 0)
        col_ids = lax.broadcasted_iota(jnp.int32, (ROWS, ROWS), 1)
        earlier = jnp.where(row_ids < col_ids, 1.0, 0.0).astype(jnp.bfloat16)
        slots = row_ids.astype(jnp.float32)
        for e in range(EXPERTS):
            mine = pick(e, 1.0, 1.0)
            before = jnp.dot(mine.astype(jnp.bfloat16), earlier, preferred_element_type=jnp.float32)
            placed = jnp.where(before == slots, mine, 0.0)
            hot[e] = placed.astype(jnp.bfloat16)
        wait(arrived, p1r)
        block = arrived[...].astype(jnp.float32).reshape(ROWS, 2 * share).astype(jnp.bfloat16)
        every = hot[:, :CAP, :].reshape(EXPERTS * CAP, ROWS)
        for i in range(2):
            packed[i] = jnp.dot(
                every, block[:, i * share:(i + 1) * share], preferred_element_type=jnp.float32
            ).reshape(EXPERTS, CAP, share).astype(jnp.bfloat16)
        for j, k in ((0, 0), (0, 1), (2, 1), (3, 0), (3, 1), (2, 0), (1, 1), (1, 0)):
            to = ring(z - turn * OFFSETS[0][j], NZ) if k == 0 else ring(z + turn * OFFSETS[1][j], NZ)
            src = packed.at[j // 2, to // (NZ // EXPERTS)]
            slot = k * BLOCKS + j
            if slot == 0:
                pltpu.make_async_copy(src, rows.at[j, center(j)], p3r.at[j]).start()
            else:
                send(src, rows.at[j, center(j)], p3s.at[slot], p3r.at[j], at(to, y, c))

    def short(rings, j, way):
        return len(rings[j][way]) == 2

    waited = set()

    def need(kind, j, *where):
        key = (kind, j) + where
        if key in waited:
            return
        waited.add(key)
        if kind == "p3":
            wait(rows.at[j, center(j)], p3r.at[j])
        elif kind == "ag":
            way, d = where
            wait(rows.at[j, near(j, way, -d)], agr.at[j, way, d - 1])
        elif kind == "zc":
            wait(rows.at[j, center(j ^ 2)], zcr.at[j, 0])
        elif kind == "zf":
            wait(rows.at[j, near(j ^ 2, HEAVY[j], -1)], zcr.at[j, 1])
        elif kind == "zg":
            wait(rows.at[j, near(j ^ 2, 1 - HEAVY[j], -1)], zcr.at[j, 2])
        elif kind == "rs":
            way, d = where
            wait(coming.at[j, way, d - 1], rsr.at[j, way, d - 1])
        else:
            wait(coming_z.at[j, where[0]], zsr.at[j, where[0]])

    def gather(j, way, d):
        parent = ag[j][way][d - 1]
        piece = rows.at[j, near(j, way, -parent)]
        need("ag", j, way, parent) if parent else need("p3", j)
        to = ring(y + (1 - 2 * way) * (d - parent), NY)
        send(piece, piece, ags.at[j, way, d - 1], agr.at[j, way, d - 1], at(z, to, c))

    def share_center(j):
        need("p3", j)
        f = center(j)
        send(rows.at[j, f], rows.at[j ^ 2, f], zcs.at[j, 0], zcr.at[j ^ 2, 0], at(partner, y, c))

    def share_near(j, way, i):
        need("ag", j, way, 1)
        f = near(j, way, -1)
        send(rows.at[j, f], rows.at[j ^ 2, f], zcs.at[j, i], zcr.at[j ^ 2, i], at(partner, y, c))

    def up(g, core):
        if core == 0:
            for j in groups[g]:
                need("p3", j)
                for way in range(2):
                    for d in range(1, len(ag[j][way]) + 1):
                        need("ag", j, way, d)
                need("zc", j)
                if short(ag, j, 1 - HEAVY[j]):
                    need("zf", j)
                if short(ag, j, HEAVY[j]):
                    need("zg", j)
        if "up" not in waited:
            waited.add("up")
            for i, (src, dst) in enumerate(weights[:2]):
                wait(dst.at[c], lw.at[i])
                wait(dst.at[1 - c], wr.at[i])
        x = jnp.concatenate(
            [jnp.concatenate([rows[j, f] for f in range(NY)], axis=1) for j in groups[g]], axis=0
        )
        gp = jnp.dot(x, gate_w[core], preferred_element_type=jnp.float32)
        u = jnp.dot(x, up_w[core], preferred_element_type=jnp.float32)
        n = gp.shape[1]
        hid = (gp / (1.0 + jnp.exp(-gp)) * u).astype(jnp.bfloat16)
        for i, j in enumerate(groups[g]):
            hidden[j, :, core * n:(core + 1) * n] = hid[i * CAP:(i + 1) * CAP]

    def down(g, half):
        if "down" not in waited:
            waited.add("down")
            wait(down_w.at[c], lw.at[2])
            wait(down_w.at[1 - c], wr.at[2])
        n = down_w.shape[1]
        h = jnp.concatenate([hidden[j] for j in groups[g]], axis=0)
        for f in range(half * NY // 2, (half + 1) * NY // 2, 2):
            lo, hi = f * share, (f + 2) * share
            r = jnp.dot(h[:, :n], down_w[0, :, lo:hi], preferred_element_type=jnp.float32)
            r += jnp.dot(h[:, n:], down_w[1, :, lo:hi], preferred_element_type=jnp.float32)
            for i, j in enumerate(groups[g]):
                partial[j, f] = r[i * CAP:(i + 1) * CAP, :share]
                partial[j, f + 1] = r[i * CAP:(i + 1) * CAP, share:]

    def across(j, i):
        f = center(j ^ 2) if i == 1 else near(j ^ 2, HEAVY[j] if i == 0 else 1 - HEAVY[j], 1)
        leaving_z[j, i] = partial[j, f].astype(jnp.bfloat16)
        send(leaving_z.at[j, i], coming_z.at[j ^ 2, i], zss.at[j, i], zsr.at[j ^ 2, i], at(partner, y, c))

    def scatter(j, way, d):
        total = partial[j, near(j, way, d)]
        if d == 1 and short(rs, j, 1 - way):
            i = 0 if way == HEAVY[j] else 2
            need("zs", j, i)
            total = total + coming_z[j, i].astype(jnp.float32)
        total = total + children(j, way, d)
        leaving[j, way, d - 1] = total.astype(jnp.bfloat16)
        to = ring(y + (1 - 2 * way) * (d - rs[j][way][d - 1]), NY)
        send(
            leaving.at[j, way, d - 1], coming.at[j, way, d - 1], rss.at[j, way, d - 1], rsr.at[j, way, d - 1],
            at(z, to, c),
        )

    def children(j, way, d):
        total = 0.0
        for e, parent in enumerate(rs[j][way], 1):
            if parent == d:
                need("rs", j, way, e)
                total = total + coming[j, way, e - 1].astype(jnp.float32)
        return total

    def finish(j):
        need("zs", j, 1)
        total = partial[j, center(j)] + coming_z[j, 1].astype(jnp.float32)
        for way in range(2):
            total = total + children(j, way, 0)
        summed[j] = total.astype(jnp.bfloat16)
        back = ring(z + turn * (OFFSETS[0][j] + side * (OFFSETS[1][j] - OFFSETS[0][j])), NZ)
        if j == 0:
            @pl.when(is_home)
            def _():
                pltpu.make_async_copy(summed.at[j], returned.at[z], rtr.at[z]).start()

            @pl.when(jnp.logical_not(is_home))
            def _():
                send(summed.at[j], returned.at[z], rts.at[j], rtr.at[z], at(back, y, c))
        else:
            send(summed.at[j], returned.at[z], rts.at[j], rtr.at[z], at(back, y, c))

    def prepare():
        @pl.when(is_home)
        def _():
            row_ids = lax.broadcasted_iota(jnp.int32, (ROWS, ROWS), 0)
            col_ids = lax.broadcasted_iota(jnp.int32, (ROWS, ROWS), 1)
            g0, g1 = (jnp.broadcast_to(gates[k:k + 1, :], (ROWS, ROWS)) for k in range(2))
            for e in range(EXPERTS):
                back_hot[e] = hot[e].astype(jnp.float32).T.astype(jnp.bfloat16)
                gate = jnp.sum(jnp.where(row_ids == col_ids, pick(e, g0, g1), 0.0), axis=1, keepdims=True)
                weight[e] = jnp.broadcast_to(gate, (ROWS, 128))

    step = {
        "zf": lambda j: share_near(j, HEAVY[j], 1), "zg": lambda j: share_near(j, 1 - HEAVY[j], 2),
        "zs": lambda j: across(j, 0), "zt": lambda j: across(j, 1), "zu": lambda j: across(j, 2), "prep": prepare,
        "ag": gather, "zc": share_center, "up": up, "down": down, "rs": scatter, "fin": finish}
    for task in order:
        step[task[0]](*task[1:])

    for dy in range(1, NY):
        wait(shares.at[0], p1s.at[dy])
    for i, (src, dst) in enumerate(weights):
        wait(src.at[0], ws.at[i])
    for j in range(BLOCKS):
        for way in range(2):
            for h in range(len(ag[j][way])):
                wait(rows.at[j, 0], ags.at[j, way, h])
            for h in range(len(rs[j][way])):
                wait(leaving.at[j, way, h], rss.at[j, way, h])
        for i, way in enumerate((None, 1 - HEAVY[j], HEAVY[j])):
            if way is None or short(ag, j, way):
                wait(rows.at[j, 0], zcs.at[j, i])
        for i, way in enumerate((1 - HEAVY[j], None, HEAVY[j])):
            if way is None or short(rs, j, way):
                wait(leaving_z.at[j, i], zss.at[j, i])

    @pl.when(is_home)
    def _():
        for i in range(1, 2 * BLOCKS):
            wait(packed.at[0, 0], p3s.at[i])

    @pl.when(jnp.logical_not(is_home))
    def _():
        wait(shares.at[0], p1s.at[0])

    @pl.when(is_home)
    def _():
        totals = [jnp.zeros((ROWS, share), jnp.float32)] * 2
        for j in [task[1] for task in order if task[0] == "fin"]:
            for k in range(2):
                to = ring(z - turn * OFFSETS[0][j], NZ) if k == 0 else ring(z + turn * OFFSETS[1][j], NZ)
                e = to // (NZ // EXPERTS)
                wait(returned.at[to], rtr.at[to])
                picked = jnp.dot(back_hot[e, :, :CAP], returned[to], preferred_element_type=jnp.float32)
                totals[j // 2] += jnp.concatenate([weight[e]] * (share // 128), axis=1) * picked
        for i in range(2):
            mixed[:, :, i * share:(i + 1) * share] = totals[i].reshape(
                NY * NC, ROWS // (NY * NC), share
            ).astype(jnp.bfloat16)
        for dy in (4, 3, 5, 2, 6, 1, 7, 0):
            for dc in range(NC):
                to, core = ring(y + dy, NY), ring(c + dc, NC)
                src = mixed.at[to * NC + core]
                if dy == 0 and dc == 0:
                    pltpu.make_async_copy(src, owned.at[y], fr).start()
                else:
                    send(src, owned.at[y], fs.at[dy * NC + dc], fr, at(z, to, core))

    wait(summed.at[1], rts.at[1])
    wait(summed.at[2], rts.at[2])
    wait(summed.at[3], rts.at[3])

    @pl.when(is_home)
    def _():
        for i in range(1, NY * NC):
            wait(mixed.at[0], fs.at[i])

    @pl.when(jnp.logical_not(is_home))
    def _():
        wait(summed.at[0], rts.at[0])

    wait(owned, fr)
    for f in range(NY):
        both = owned[f, :, :share].astype(jnp.float32)
        both += owned[(f + NY // 2) % NY, :, share:].astype(jnp.float32)
        out[:, f * share:(f + 1) * share] = both.astype(jnp.bfloat16)


def local(tokens, routes, gates, w_gate, w_up, w_down):
    tok_dev, width = tokens.shape
    hid = w_gate.shape[2]
    share = width // NY
    bf16, f32 = jnp.bfloat16, jnp.float32
    dma = pltpu.SemaphoreType.DMA
    hbm = pl.BlockSpec(memory_space=pltpu.HBM)
    return pl.pallas_call(
        kernel,
        out_shape=jax.ShapeDtypeStruct((tok_dev, width), bf16),
        in_specs=[hbm] * 6,
        out_specs=pl.BlockSpec(memory_space=pltpu.VMEM),
        scratch_shapes=[
            pltpu.VMEM((tok_dev, width), bf16),
            pltpu.VMEM((NY, tok_dev, 2 * share), bf16),
            pltpu.VMEM((2, ROWS), jnp.int32),
            pltpu.VMEM((2, ROWS), f32),
            pltpu.VMEM((NY * NC, tok_dev, 2 * share), bf16),
            pltpu.VMEM((NC, width, hid), bf16),
            pltpu.VMEM((NC, width, hid), bf16),
            pltpu.VMEM((NC, hid, width), bf16),
            pltpu.VMEM((EXPERTS, ROWS, ROWS), bf16),
            pltpu.VMEM((EXPERTS, ROWS, ROWS), bf16),
            pltpu.VMEM((EXPERTS, ROWS, 128), f32),
            pltpu.VMEM((2, EXPERTS, CAP, share), bf16),
            pltpu.VMEM((BLOCKS, NY, CAP, share), bf16),
            pltpu.VMEM((BLOCKS, CAP, NC * hid), bf16),
            pltpu.VMEM((BLOCKS, NY, CAP, share), f32),
            pltpu.VMEM((BLOCKS, 2, 3, CAP, share), bf16),
            pltpu.VMEM((BLOCKS, 2, 3, CAP, share), bf16),
            pltpu.VMEM((BLOCKS, 3, CAP, share), bf16),
            pltpu.VMEM((BLOCKS, 3, CAP, share), bf16),
            pltpu.VMEM((BLOCKS, CAP, share), bf16),
            pltpu.VMEM((NZ, CAP, share), bf16),
            pltpu.VMEM((NY * NC, tok_dev, 2 * share), bf16),
            pltpu.VMEM((NY, tok_dev, 2 * share), bf16),
            dma((NY,)), dma,
            dma((6,)), dma((3,)), dma((3,)),
            dma((2 * BLOCKS,)), dma((BLOCKS,)),
            dma((BLOCKS, 2, 3)), dma((BLOCKS, 2, 3)),
            dma((BLOCKS, 3)), dma((BLOCKS, 3)),
            dma((BLOCKS, 2, 3)), dma((BLOCKS, 2, 3)),
            dma((BLOCKS, 3)), dma((BLOCKS, 3)),
            dma((BLOCKS,)), dma((NZ,)),
            dma((NY * NC,)), dma,
        ],
        compiler_params=pltpu.CompilerParams(
            collective_id=0, has_side_effects=True, vmem_limit_bytes=62 * 2**20
        ),
        name="moe",
    )(tokens, routes.T, gates.T, w_gate, w_up, w_down)


def solution(mesh):
    return jax.shard_map(
        local,
        mesh=mesh,
        in_specs=(
            P(("dp", "exp", "tp"), None),
            P(("dp", "exp"), None),
            P(("dp", "exp"), None),
            P("exp", None, "tp"),
            P("exp", None, "tp"),
            P("exp", "tp", None),
        ),
        out_specs=P(("dp", "exp", "tp"), None),
        check_vma=False,
    )
```

```python
import jax
import jax.numpy as jnp
from jax import lax
from jax.experimental import pallas as pl
from jax.experimental.pallas import tpu as pltpu
from jax.sharding import PartitionSpec as P

MESH = pl.DeviceIdType.MESH
EXPERTS = 4
NZ = 8
NY = 8
NC = 2
ROWS = 128
CAP = 80
BLOCKS = NZ // NC
OFFSETS = ((0, 2, -2, 4), (1, 3, -1, -3))


HEAVY = (0, 1, 0, 1)


GROUPS = ((1, 3), (0, 2))
GATHER = (((0, 1, 2), (0, 1)), ((0, 1), (0, 1, 2)), ((0, 1, 2), (0, 1)), ((0, 1), (0, 1, 2)))
SCATTER = (((0, 1, 2), (0, 1)), ((0, 1), (0, 1, 2)), ((0, 1, 2), (0, 1)), ((0, 1), (0, 1, 2)))
ORDER = (
    ("ag", 3, 0, 1),
    ("zc", 3),
    ("ag", 3, 1, 1),
    ("ag", 0, 0, 1),
    ("zc", 0),
    ("ag", 0, 1, 1),
    ("ag", 1, 1, 1),
    ("ag", 1, 0, 1),
    ("ag", 2, 0, 1),
    ("zc", 1),
    ("zf", 3),
    ("ag", 3, 0, 2),
    ("ag", 3, 1, 2),
    ("ag", 2, 1, 1),
    ("zf", 0),
    ("ag", 1, 1, 2),
    ("prep",),
    ("ag", 0, 0, 2),
    ("zf", 1),
    ("ag", 3, 1, 3),
    ("ag", 2, 0, 2),
    ("ag", 1, 0, 2),
    ("zf", 2),
    ("ag", 1, 1, 3),
    ("ag", 0, 0, 3),
    ("ag", 0, 1, 2),
    ("zc", 2),
    ("ag", 2, 0, 3),
    ("ag", 2, 1, 2),
    ("up", 0, 0),
    ("up", 0, 1),
    ("down", 0, 0),
    ("down", 0, 1),
    ("rs", 3, 1, 3),
    ("rs", 1, 0, 2),
    ("zs", 3),
    ("rs", 3, 0, 2),
    ("rs", 1, 1, 3),
    ("zt", 1),
    ("zs", 1),
    ("up", 1, 0),
    ("up", 1, 1),
    ("down", 1, 0),
    ("rs", 3, 1, 2),
    ("down", 1, 1),
    ("rs", 0, 0, 3),
    ("rs", 2, 0, 3),
    ("rs", 2, 1, 2),
    ("rs", 1, 0, 1),
    ("rs", 1, 1, 2),
    ("zt", 3),
    ("zs", 2),
    ("rs", 3, 0, 1),
    ("rs", 0, 1, 2),
    ("rs", 3, 1, 1),
    ("zs", 0),
    ("zt", 2),
    ("rs", 2, 0, 2),
    ("rs", 0, 0, 2),
    ("rs", 1, 1, 1),
    ("zt", 0),
    ("rs", 2, 1, 1),
    ("rs", 0, 1, 1),
    ("rs", 2, 0, 1),
    ("fin", 3),
    ("rs", 0, 0, 1),
    ("fin", 1),
    ("fin", 2),
    ("fin", 0),
)


def kernel(
    tok_in, routes_in, gates_in, wg, wu, wd, out,
    tok, shares, routes, gates, arrived, gate_w, up_w, down_w, hot, back_hot, weight, packed, rows, hidden, partial,
    leaving, coming, leaving_z, coming_z, summed, returned, mixed, owned,
    p1s, p1r, lw, ws, wr, p3s, p3r, ags, agr, zcs, zcr, rss, rsr, zss, zsr, rts, rtr, fs, fr,
):
    groups, ag, rs, order = GROUPS, GATHER, SCATTER, ORDER
    z = lax.axis_index("exp")
    t = lax.axis_index("tp")
    y = t // NC
    c = lax.rem(t, NC)
    home_core = lax.rem(z, NC)
    side = lax.rem(z + c, NC)
    is_home = side == 0
    turn = 2 * home_core - 1
    share = rows.shape[-1]

    def at(zz, yy, cc):
        return {"exp": zz, "tp": yy * NC + cc}

    def ring(v, n):
        return lax.rem(v + n, n)

    def send(src, dst, ssem, rsem, device):
        pltpu.make_async_remote_copy(
            src_ref=src, dst_ref=dst, send_sem=ssem, recv_sem=rsem, device_id=device, device_id_type=MESH
        ).start()

    def wait(ref, sem):
        pltpu.make_async_copy(ref, ref, sem).wait()

    def chunk(ref, index):
        return ref.at[:, pl.ds(pl.multiple_of(index * share, 128), share)]

    def center(j):
        return ring(y + j // 2 * (NY // 2), NY)

    def near(j, way, d):
        return ring(center(j) + (1 - 2 * way) * d, NY)

    partner = z - turn
    weights = ((wg, gate_w), (wu, up_w), (wd, down_w))
    small = ((tok_in, tok), (routes_in, routes), (gates_in, gates))
    barrier = pltpu.get_barrier_semaphore()
    for d in (4, 3, 5, 2, 6, 1, 7, 0):
        peers = [at(z, ring(y + d, NY), c), at(z, ring(y + d, NY), 1 - c), at(ring(z + d, NZ), y, c)]
        for peer in peers if d else peers[1:2]:
            pl.semaphore_signal(barrier, inc=1, device_id=peer, device_id_type=MESH)
    for i, (src, dst) in enumerate(small):
        pltpu.make_async_copy(src, dst, lw.at[3 + i]).start()
    for i, (src, dst) in enumerate(weights):
        pltpu.make_async_copy(src.at[0], dst.at[c], lw.at[i]).start()
    wait(tok, lw.at[3])
    for f in range(NY):
        g = (f + NY // 2) % NY
        shares[f, :, :share] = tok[:, f * share:(f + 1) * share]
        shares[f, :, share:] = tok[:, g * share:(g + 1) * share]
    pl.semaphore_wait(barrier, NY * NC - 1 + NZ - 1)

    for dy in (4, 3, 5, 2, 6, 1, 7):
        to = ring(y + dy, NY)
        send(shares.at[to], arrived.at[t], p1s.at[dy], p1r, at(z, to, home_core))

    @pl.when(is_home)
    def _():
        pltpu.make_async_copy(shares.at[y], arrived.at[t], p1r).start()

    @pl.when(jnp.logical_not(is_home))
    def _():
        send(shares.at[y], arrived.at[t], p1s.at[0], p1r, at(z, y, home_core))

    for i, (src, dst) in enumerate(weights):
        send(src.at[0], dst.at[c], ws.at[i], wr.at[i], at(z, y, 1 - c))

    for i, (src, dst) in enumerate(small[1:]):
        wait(dst, lw.at[4 + i])

    def pick(e, first, second):
        here = [jnp.broadcast_to(routes[k:k + 1, :], (ROWS, ROWS)) == e for k in range(2)]
        return jnp.where(here[0], first, 0.0) + jnp.where(here[1], second, 0.0)

    @pl.when(is_home)
    def _():
        row_ids = lax.broadcasted_iota(jnp.int32, (ROWS, ROWS), 0)
        col_ids = lax.broadcasted_iota(jnp.int32, (ROWS, ROWS), 1)
        earlier = jnp.where(row_ids < col_ids, 1.0, 0.0).astype(jnp.bfloat16)
        slots = row_ids.astype(jnp.float32)
        for e in range(EXPERTS):
            mine = pick(e, 1.0, 1.0)
            before = jnp.dot(mine.astype(jnp.bfloat16), earlier, preferred_element_type=jnp.float32)
            placed = jnp.where(before == slots, mine, 0.0)
            hot[e] = placed.astype(jnp.bfloat16)
        wait(arrived, p1r)
        block = arrived[...].astype(jnp.float32).reshape(ROWS, 2 * share).astype(jnp.bfloat16)
        every = hot[:, :CAP, :].reshape(EXPERTS * CAP, ROWS)
        for i in range(2):
            packed[i] = jnp.dot(
                every, block[:, i * share:(i + 1) * share], preferred_element_type=jnp.float32
            ).reshape(EXPERTS, CAP, share).astype(jnp.bfloat16)
        for j, k in ((0, 0), (3, 0), (3, 1), (1, 1), (1, 0), (2, 0), (0, 1), (2, 1)):
            to = ring(z - turn * OFFSETS[0][j], NZ) if k == 0 else ring(z + turn * OFFSETS[1][j], NZ)
            src = packed.at[j // 2, to // (NZ // EXPERTS)]
            slot = k * BLOCKS + j
            if slot == 0:
                pltpu.make_async_copy(src, rows.at[j, center(j)], p3r.at[j]).start()
            else:
                send(src, rows.at[j, center(j)], p3s.at[slot], p3r.at[j], at(to, y, c))

    def short(rings, j, way):
        return len(rings[j][way]) == 2

    waited = set()

    def need(kind, j, *where):
        key = (kind, j) + where
        if key in waited:
            return
        waited.add(key)
        if kind == "p3":
            wait(rows.at[j, center(j)], p3r.at[j])
        elif kind == "ag":
            way, d = where
            wait(rows.at[j, near(j, way, -d)], agr.at[j, way, d - 1])
        elif kind == "zc":
            wait(rows.at[j, center(j ^ 2)], zcr.at[j, 0])
        elif kind == "zf":
            wait(rows.at[j, near(j ^ 2, HEAVY[j], -1)], zcr.at[j, 1])
        elif kind == "zg":
            wait(rows.at[j, near(j ^ 2, 1 - HEAVY[j], -1)], zcr.at[j, 2])
        elif kind == "rs":
            way, d = where
            wait(coming.at[j, way, d - 1], rsr.at[j, way, d - 1])
        else:
            wait(coming_z.at[j, where[0]], zsr.at[j, where[0]])

    def gather(j, way, d):
        parent = ag[j][way][d - 1]
        piece = rows.at[j, near(j, way, -parent)]
        need("ag", j, way, parent) if parent else need("p3", j)
        to = ring(y + (1 - 2 * way) * (d - parent), NY)
        send(piece, piece, ags.at[j, way, d - 1], agr.at[j, way, d - 1], at(z, to, c))

    def share_center(j):
        need("p3", j)
        f = center(j)
        send(rows.at[j, f], rows.at[j ^ 2, f], zcs.at[j, 0], zcr.at[j ^ 2, 0], at(partner, y, c))

    def share_near(j, way, i):
        need("ag", j, way, 1)
        f = near(j, way, -1)
        send(rows.at[j, f], rows.at[j ^ 2, f], zcs.at[j, i], zcr.at[j ^ 2, i], at(partner, y, c))

    def up(g, core):
        if core == 0:
            for j in groups[g]:
                need("p3", j)
                for way in range(2):
                    for d in range(1, len(ag[j][way]) + 1):
                        need("ag", j, way, d)
                need("zc", j)
                if short(ag, j, 1 - HEAVY[j]):
                    need("zf", j)
                if short(ag, j, HEAVY[j]):
                    need("zg", j)
        if "up" not in waited:
            waited.add("up")
            for i, (src, dst) in enumerate(weights[:2]):
                wait(dst.at[c], lw.at[i])
                wait(dst.at[1 - c], wr.at[i])
        x = jnp.concatenate(
            [jnp.concatenate([rows[j, f] for f in range(NY)], axis=1) for j in groups[g]], axis=0
        )
        gp = jnp.dot(x, gate_w[core], preferred_element_type=jnp.float32)
        u = jnp.dot(x, up_w[core], preferred_element_type=jnp.float32)
        n = gp.shape[1]
        hid = (gp / (1.0 + jnp.exp(-gp)) * u).astype(jnp.bfloat16)
        for i, j in enumerate(groups[g]):
            hidden[j, :, core * n:(core + 1) * n] = hid[i * CAP:(i + 1) * CAP]

    def down(g, half):
        if "down" not in waited:
            waited.add("down")
            wait(down_w.at[c], lw.at[2])
            wait(down_w.at[1 - c], wr.at[2])
        n = down_w.shape[1]
        h = jnp.concatenate([hidden[j] for j in groups[g]], axis=0)
        for f in range(half * NY // 2, (half + 1) * NY // 2, 2):
            lo, hi = f * share, (f + 2) * share
            r = jnp.dot(h[:, :n], down_w[0, :, lo:hi], preferred_element_type=jnp.float32)
            r += jnp.dot(h[:, n:], down_w[1, :, lo:hi], preferred_element_type=jnp.float32)
            for i, j in enumerate(groups[g]):
                partial[j, f] = r[i * CAP:(i + 1) * CAP, :share]
                partial[j, f + 1] = r[i * CAP:(i + 1) * CAP, share:]

    def across(j, i):
        f = center(j ^ 2) if i == 1 else near(j ^ 2, HEAVY[j] if i == 0 else 1 - HEAVY[j], 1)
        leaving_z[j, i] = partial[j, f].astype(jnp.bfloat16)
        send(leaving_z.at[j, i], coming_z.at[j ^ 2, i], zss.at[j, i], zsr.at[j ^ 2, i], at(partner, y, c))

    def scatter(j, way, d):
        total = partial[j, near(j, way, d)]
        if d == 1 and short(rs, j, 1 - way):
            i = 0 if way == HEAVY[j] else 2
            need("zs", j, i)
            total = total + coming_z[j, i].astype(jnp.float32)
        total = total + children(j, way, d)
        leaving[j, way, d - 1] = total.astype(jnp.bfloat16)
        to = ring(y + (1 - 2 * way) * (d - rs[j][way][d - 1]), NY)
        send(
            leaving.at[j, way, d - 1], coming.at[j, way, d - 1], rss.at[j, way, d - 1], rsr.at[j, way, d - 1],
            at(z, to, c),
        )

    def children(j, way, d):
        total = 0.0
        for e, parent in enumerate(rs[j][way], 1):
            if parent == d:
                need("rs", j, way, e)
                total = total + coming[j, way, e - 1].astype(jnp.float32)
        return total

    def finish(j):
        need("zs", j, 1)
        total = partial[j, center(j)] + coming_z[j, 1].astype(jnp.float32)
        for way in range(2):
            total = total + children(j, way, 0)
        summed[j] = total.astype(jnp.bfloat16)
        back = ring(z + turn * (OFFSETS[0][j] + side * (OFFSETS[1][j] - OFFSETS[0][j])), NZ)
        if j == 0:
            @pl.when(is_home)
            def _():
                pltpu.make_async_copy(summed.at[j], returned.at[z], rtr.at[z]).start()

            @pl.when(jnp.logical_not(is_home))
            def _():
                send(summed.at[j], returned.at[z], rts.at[j], rtr.at[z], at(back, y, c))
        else:
            send(summed.at[j], returned.at[z], rts.at[j], rtr.at[z], at(back, y, c))

    def prepare():
        @pl.when(is_home)
        def _():
            row_ids = lax.broadcasted_iota(jnp.int32, (ROWS, ROWS), 0)
            col_ids = lax.broadcasted_iota(jnp.int32, (ROWS, ROWS), 1)
            g0, g1 = (jnp.broadcast_to(gates[k:k + 1, :], (ROWS, ROWS)) for k in range(2))
            for e in range(EXPERTS):
                back_hot[e] = hot[e].astype(jnp.float32).T.astype(jnp.bfloat16)
                gate = jnp.sum(jnp.where(row_ids == col_ids, pick(e, g0, g1), 0.0), axis=1, keepdims=True)
                weight[e] = jnp.broadcast_to(gate, (ROWS, 128))

    step = {
        "zf": lambda j: share_near(j, HEAVY[j], 1), "zg": lambda j: share_near(j, 1 - HEAVY[j], 2),
        "zs": lambda j: across(j, 0), "zt": lambda j: across(j, 1), "zu": lambda j: across(j, 2), "prep": prepare,
        "ag": gather, "zc": share_center, "up": up, "down": down, "rs": scatter, "fin": finish}
    for task in order:
        step[task[0]](*task[1:])

    for dy in range(1, NY):
        wait(shares.at[0], p1s.at[dy])
    for i, (src, dst) in enumerate(weights):
        wait(src.at[0], ws.at[i])
    for j in range(BLOCKS):
        for way in range(2):
            for h in range(len(ag[j][way])):
                wait(rows.at[j, 0], ags.at[j, way, h])
            for h in range(len(rs[j][way])):
                wait(leaving.at[j, way, h], rss.at[j, way, h])
        for i, way in enumerate((None, 1 - HEAVY[j], HEAVY[j])):
            if way is None or short(ag, j, way):
                wait(rows.at[j, 0], zcs.at[j, i])
        for i, way in enumerate((1 - HEAVY[j], None, HEAVY[j])):
            if way is None or short(rs, j, way):
                wait(leaving_z.at[j, i], zss.at[j, i])

    @pl.when(is_home)
    def _():
        for i in range(1, 2 * BLOCKS):
            wait(packed.at[0, 0], p3s.at[i])

    @pl.when(jnp.logical_not(is_home))
    def _():
        wait(shares.at[0], p1s.at[0])

    @pl.when(is_home)
    def _():
        totals = [jnp.zeros((ROWS, share), jnp.float32)] * 2
        for j in [task[1] for task in order if task[0] == "fin"]:
            for k in range(2):
                to = ring(z - turn * OFFSETS[0][j], NZ) if k == 0 else ring(z + turn * OFFSETS[1][j], NZ)
                e = to // (NZ // EXPERTS)
                wait(returned.at[to], rtr.at[to])
                picked = jnp.dot(back_hot[e, :, :CAP], returned[to], preferred_element_type=jnp.float32)
                totals[j // 2] += jnp.concatenate([weight[e]] * (share // 128), axis=1) * picked
        for i in range(2):
            mixed[:, :, i * share:(i + 1) * share] = totals[i].reshape(
                NY * NC, ROWS // (NY * NC), share
            ).astype(jnp.bfloat16)
        for dy in (4, 3, 5, 2, 6, 1, 7, 0):
            for dc in range(NC):
                to, core = ring(y + dy, NY), ring(c + dc, NC)
                src = mixed.at[to * NC + core]
                if dy == 0 and dc == 0:
                    pltpu.make_async_copy(src, owned.at[y], fr).start()
                else:
                    send(src, owned.at[y], fs.at[dy * NC + dc], fr, at(z, to, core))

    wait(summed.at[1], rts.at[1])
    wait(summed.at[2], rts.at[2])
    wait(summed.at[3], rts.at[3])

    @pl.when(is_home)
    def _():
        for i in range(1, NY * NC):
            wait(mixed.at[0], fs.at[i])

    @pl.when(jnp.logical_not(is_home))
    def _():
        wait(summed.at[0], rts.at[0])

    wait(owned, fr)
    for f in range(NY):
        both = owned[f, :, :share].astype(jnp.float32)
        both += owned[(f + NY // 2) % NY, :, share:].astype(jnp.float32)
        out[:, f * share:(f + 1) * share] = both.astype(jnp.bfloat16)


def local(tokens, routes, gates, w_gate, w_up, w_down):
    tok_dev, width = tokens.shape
    hid = w_gate.shape[2]
    share = width // NY
    bf16, f32 = jnp.bfloat16, jnp.float32
    dma = pltpu.SemaphoreType.DMA
    hbm = pl.BlockSpec(memory_space=pltpu.HBM)
    return pl.pallas_call(
        kernel,
        out_shape=jax.ShapeDtypeStruct((tok_dev, width), bf16),
        in_specs=[hbm] * 6,
        out_specs=pl.BlockSpec(memory_space=pltpu.VMEM),
        scratch_shapes=[
            pltpu.VMEM((tok_dev, width), bf16),
            pltpu.VMEM((NY, tok_dev, 2 * share), bf16),
            pltpu.VMEM((2, ROWS), jnp.int32),
            pltpu.VMEM((2, ROWS), f32),
            pltpu.VMEM((NY * NC, tok_dev, 2 * share), bf16),
            pltpu.VMEM((NC, width, hid), bf16),
            pltpu.VMEM((NC, width, hid), bf16),
            pltpu.VMEM((NC, hid, width), bf16),
            pltpu.VMEM((EXPERTS, ROWS, ROWS), bf16),
            pltpu.VMEM((EXPERTS, ROWS, ROWS), bf16),
            pltpu.VMEM((EXPERTS, ROWS, 128), f32),
            pltpu.VMEM((2, EXPERTS, CAP, share), bf16),
            pltpu.VMEM((BLOCKS, NY, CAP, share), bf16),
            pltpu.VMEM((BLOCKS, CAP, NC * hid), bf16),
            pltpu.VMEM((BLOCKS, NY, CAP, share), f32),
            pltpu.VMEM((BLOCKS, 2, 3, CAP, share), bf16),
            pltpu.VMEM((BLOCKS, 2, 3, CAP, share), bf16),
            pltpu.VMEM((BLOCKS, 3, CAP, share), bf16),
            pltpu.VMEM((BLOCKS, 3, CAP, share), bf16),
            pltpu.VMEM((BLOCKS, CAP, share), bf16),
            pltpu.VMEM((NZ, CAP, share), bf16),
            pltpu.VMEM((NY * NC, tok_dev, 2 * share), bf16),
            pltpu.VMEM((NY, tok_dev, 2 * share), bf16),
            dma((NY,)), dma,
            dma((6,)), dma((3,)), dma((3,)),
            dma((2 * BLOCKS,)), dma((BLOCKS,)),
            dma((BLOCKS, 2, 3)), dma((BLOCKS, 2, 3)),
            dma((BLOCKS, 3)), dma((BLOCKS, 3)),
            dma((BLOCKS, 2, 3)), dma((BLOCKS, 2, 3)),
            dma((BLOCKS, 3)), dma((BLOCKS, 3)),
            dma((BLOCKS,)), dma((NZ,)),
            dma((NY * NC,)), dma,
        ],
        compiler_params=pltpu.CompilerParams(
            collective_id=0, has_side_effects=True, vmem_limit_bytes=62 * 2**20
        ),
        name="moe",
    )(tokens, routes.T, gates.T, w_gate, w_up, w_down)


def solution(mesh):
    return jax.shard_map(
        local,
        mesh=mesh,
        in_specs=(
            P(("dp", "exp", "tp"), None),
            P(("dp", "exp"), None),
            P(("dp", "exp"), None),
            P("exp", None, "tp"),
            P("exp", None, "tp"),
            P("exp", "tp", None),
        ),
        out_specs=P(("dp", "exp", "tp"), None),
        check_vma=False,
    )
```
